256 devices in a mesh: ctx: 16 (over y_hi, x, core), ch: 16 (over y_lo, z).
Axes of the slice: x: 4, y: 4 (y_hi: 2, y_lo: 2; y = y_hi * 2 + y_lo), z: 8, core: 2. Of those that a mesh axis runs over, the one named last changes fastest.
Arguments:
- streams: bfloat16 [3, 24576, 4096], P(None, 'ctx', 'ch'), may hold values from -6 to 6
- taps: float32 [3, 3, 4096], P(None, None, 'ch'), may hold values from -4 to 4
- residues: float32 [4096, 16], P('ch'), may hold values from -4 to 4
- decay: float32 [4096, 16], P('ch'), may hold values from 8.138021e-06 to 0.03
- skip: float32 [4096], P('ch'), may hold values from 0.5 to 1.5
- w_out: bfloat16 [4096, 4096], P('ch', 'ctx'), may hold values from -0.125 to 0.125
Outputs:
- layer_out: bfloat16 [24576, 4096], P('ctx', 'ch')
The draws below stay inside these ranges and needn't reach their ends.
All inputs are finite; a program needn't handle non-finite values.
Results may differ from the reference program's by a relative error of at most 0.0049.
Values may be sent and summed in bfloat16 or wider, within the bound.
No kernel may reach another device: no remote copies, remote signals or barrier semaphores. Data moves between devices by JAX's collectives and lax.ppermute only.
A program may use at most 128 MiB of HBM per device.

```python
import jax
import jax.numpy as jnp
from jax import lax

D = 4096
MODES = 16
TOKENS = 24576


def draw_decay(key, part):
    key = jax.random.fold_in(key, 5)
    return jnp.exp(jax.random.uniform(key, (D, MODES), jnp.float32, jnp.log(0.2 / TOKENS), jnp.log(0.03)))


def strengthened(values, own_key, source, target, blocks, factor):
    def block_of(dim):
        return (jnp.arange(values.shape[dim]) // (values.shape[dim] // blocks)).reshape((-1,) + (1,) * (values.ndim - 1 - dim))

    first = jax.random.permutation(own_key, blocks)[block_of(target)]
    far = (block_of(target) + blocks // 2) % blocks
    return jnp.where((block_of(source) == first) | (block_of(source) == far), factor * values, values)


def level_of(key, shape, shards, least, largest):
    def one(dim, shards_of):
        heights = jax.random.uniform(jax.random.fold_in(jax.random.fold_in(key, 6), dim), (shards_of,), jnp.float32, least / len(shards), largest / len(shards))
        return jnp.repeat(jnp.exp(heights), shape[dim] // shards_of).reshape((-1,) + (1,) * (len(shape) - dim - 1))

    loudness = one(*shards[0])
    for cut in shards[1:]:
        loudness = loudness * one(*cut)
    return loudness


def centred(stream_key, dims, spread, limit, shards=(), held_as=jnp.bfloat16):
    entries = jax.random.normal(stream_key, dims, jnp.float32) * spread
    if len(shards) > 0:
        entries = level_of(stream_key, dims, shards, -0.22, 0.18) * entries
    return jnp.clip(entries, min=-limit, max=limit).astype(held_as)


def gaussian_with(key, dims, spread, reach, cuts, heavy, dtype=jnp.bfloat16):
    result = spread * jax.random.normal(key, dims, jnp.float32)
    if cuts:
        result = result * level_of(key, dims, cuts, -0.22, 0.18)
    return jnp.clip(strengthened(result, jax.random.fold_in(key, 3), *heavy), -reach, reach).astype(dtype)


def setup_inputs(seed: int = 0) -> dict:
    key_of = jax.random.split(jax.random.key(seed), 7)
    return {
        "streams": centred(key_of[0], (3, TOKENS, D), 1.0, 6.0, ((1, 16), (2, 16))),
        "taps": centred(key_of[1], (3, 3, D), 0.6, 4.0, ((2, 16),), jnp.float32),
        "residues": centred(key_of[2], (D, MODES), 0.35, 4.0, ((0, 16),), jnp.float32),
        "decay": draw_decay(jax.random.fold_in(key_of[6], 71), 0),
        "skip": jnp.clip(0.5 + 1.0 * jax.random.uniform(key_of[4], (D,), jnp.float32) ** level_of(key_of[4], (D,), ((0, 16),), -0.2, 0.2), 0.5, 1.5),
        "w_out": gaussian_with(key_of[5], (D, D), D ** -0.5, 0.125, ((0, 16), (1, 16)), (0, 1, 16, 2.0)),
    }


def block_conv(args):
    drive_blk, res_blk, rate_blk = args
    length = drive_blk.shape[0]
    lags = jnp.arange(length).astype(jnp.float32)
    scaled = res_blk * jnp.sqrt(rate_blk)
    filt = jnp.zeros(drive_blk.shape, jnp.float32)
    for mode in range(MODES):
        filt = filt + scaled[:, mode][None, :] * jnp.exp(-rate_blk[:, mode][None, :] * lags[:, None])
    total = 2 * length
    spec_drive = jnp.fft.rfft(drive_blk, n=total, axis=0)
    spec_filt = jnp.fft.rfft(filt, n=total, axis=0)
    return jnp.fft.irfft(spec_drive * spec_filt, n=total, axis=0)[:length].astype(jnp.float32)

def reference(streams, taps, residues, decay, skip, w_out):
    source = streams.astype(jnp.float32)
    padded = jnp.pad(source, ((0, 0), (2, 0), (0, 0)))
    filtered = taps[:, 0, :][:, None, :] * source + taps[:, 1, :][:, None, :] * padded[:, 1:-1, :] + taps[:, 2, :][:, None, :] * padded[:, :-2, :]
    query = filtered[0]
    drive = filtered[1] * filtered[2]
    group = 256
    count = D // group
    drive_groups = jnp.transpose(drive.reshape(TOKENS, count, group), (1, 0, 2))
    conv_groups = lax.map(block_conv, (drive_groups, residues.reshape(count, group, MODES), decay.reshape(count, group, MODES)))
    conv = jnp.transpose(conv_groups, (1, 0, 2)).reshape(TOKENS, D)
    gated = (query * (conv + skip[None, :] * drive)).astype(jnp.bfloat16)
    return jnp.dot(gated, w_out, preferred_element_type=jnp.float32).astype(jnp.bfloat16)
```

```python
import functools

import jax
import jax.numpy as jnp
from jax import lax
from jax.experimental import pallas as pl
from jax.experimental.pallas import tpu as pltpu
from jax.sharding import PartitionSpec as P

MODES = 16
LANES = 128
SEGS = 8
CHUNKS = 3
CTX = 16
CH = 16
RING = 8
F32 = jnp.float32
BF16 = jnp.bfloat16
VMEM_LIMIT = 24 * 1024 * 1024


def row_ids():
    return lax.broadcasted_iota(jnp.int32, (SEGS, LANES), 0)


def wide(row):
    return jnp.broadcast_to(row, (SEGS, LANES))


def states_kernel(
    me_ref, k_ref, v_ref, halo_ref, taps_ref, decay_ref,
    drive_ref, segend_ref, start_ref, send_ref, kx, vx, ends,
):
    tokens = k_ref.shape[1]
    chunk = tokens // CHUNKS
    steps = chunk // SEGS
    kx[pl.ds(8, tokens), :] = k_ref[0].astype(F32)
    vx[pl.ds(8, tokens), :] = v_ref[0].astype(F32)
    kx[pl.ds(6, 2), :] = halo_ref[1].astype(F32)
    vx[pl.ds(6, 2), :] = halo_ref[2].astype(F32)
    decay = decay_ref[...]
    keep = jnp.exp(-decay)
    keeps = [wide(keep[m : m + 1]) for m in range(MODES)]
    tk = [wide(taps_ref[1, j : j + 1, :]) for j in range(3)]
    tv = [wide(taps_ref[2, j : j + 1, :]) for j in range(3)]
    later = (SEGS - 1 - row_ids()).astype(F32) * steps

    for c in range(CHUNKS):
        base = 8 + c * chunk

        def at(ref, i):
            return ref[pl.ds(base + i, SEGS, stride=steps), :]

        def step(i, carry):
            k1, k2, v1, v2, acc = carry
            k0, v0 = at(kx, i), at(vx, i)
            keyed = tk[0] * k0 + tk[1] * k1 + tk[2] * k2
            valued = tv[0] * v0 + tv[1] * v1 + tv[2] * v2
            drive = keyed * valued
            drive_ref[pl.ds(pl.multiple_of(c * chunk + i * SEGS, SEGS), SEGS), :] = drive
            return k0, k1, v0, v1, tuple(a * s + drive for a, s in zip(keeps, acc))

        zero = tuple(jnp.zeros((SEGS, LANES), F32) for _ in range(MODES))
        acc = lax.fori_loop(
            0, steps, step,
            (at(kx, -1), at(kx, -2), at(vx, -1), at(vx, -2), zero),
            unroll=4,
        )[4]
        for m in range(MODES):
            segend_ref[c, m] = acc[m]
            weight = jnp.exp(-wide(decay[m : m + 1]) * later)
            ends[c, pl.ds(m, 1), :] = jnp.sum(acc[m] * weight, axis=0, keepdims=True)

    state = jnp.zeros((MODES, LANES), F32)
    span = jnp.exp(-decay * chunk)
    for c in range(CHUNKS):
        start_ref[c] = state
        state = state * span + ends[c]
    me = me_ref[0]
    for j in range(CTX):
        gap = j - 1 - me
        lag = (jnp.maximum(gap, 0) * tokens).astype(F32)
        send_ref[j] = jnp.where(gap >= 0, jnp.exp(-decay * lag) * state, 0.0)


def gate_kernel(
    c, q_ref, qb_ref, taps_ref, decay_ref, res_ref, skip_ref, drive_ref, segend_ref,
    start_ref, recv_ref, out_ref, qx, gx,
):
    chunk = q_ref.shape[1]
    steps = chunk // SEGS
    qx[pl.ds(8, chunk), :] = q_ref[0].astype(F32)
    before = qb_ref[0].astype(F32)
    qx[pl.ds(6, 2), :] = before[before.shape[0] - 2 :]
    decay = decay_ref[...]
    keep = jnp.exp(-decay)
    keep1 = jnp.exp(-decay * steps)
    keep2 = jnp.exp(-decay * (2 * steps))
    keep4 = jnp.exp(-decay * (4 * steps))
    scaled = res_ref[...] * jnp.sqrt(decay)
    incoming = recv_ref[0]
    for j in range(1, CTX):
        incoming = incoming + recv_ref[j]
    entry = jnp.exp(-decay * (c * chunk)) * incoming + start_ref[0]
    rows = row_ids()
    acc = []
    for m in range(MODES):
        x = jnp.where(rows == 0, wide(entry[m : m + 1]), pltpu.roll(segend_ref[0, m], 1, 0))
        for far, factor in ((1, keep1), (2, keep2), (4, keep4)):
            moved = pltpu.roll(x, far, 0) * wide(factor[m : m + 1])
            x = x + jnp.where(rows >= far, moved, 0.0)
        acc.append(x)
    keeps = [wide(keep[m : m + 1]) for m in range(MODES)]
    gains = [wide(scaled[m : m + 1]) for m in range(MODES)]
    tq = [wide(taps_ref[0, j : j + 1, :]) for j in range(3)]
    skip = wide(skip_ref[...])

    def at(i):
        return qx[pl.ds(8 + i, SEGS, stride=steps), :]

    def step(i, carry):
        q1, q2, acc = carry
        q0 = at(i)
        drive = drive_ref[pl.ds(pl.multiple_of(i * SEGS, SEGS), SEGS), :]
        acc = tuple(a * s + drive for a, s in zip(keeps, acc))
        terms = [g * s for g, s in zip(gains, acc)] + [skip * drive]
        while len(terms) > 1:
            terms = [sum(terms[i : i + 2]) for i in range(0, len(terms), 2)]
        query = tq[0] * q0 + tq[1] * q1 + tq[2] * q2
        gx[pl.ds(i, SEGS, stride=steps), :] = query * terms[0]
        return q0, q1, acc

    lax.fori_loop(0, steps, step, (at(-1), at(-2), tuple(acc)), unroll=4)
    out_ref[...] = gx[...].astype(BF16)


def project_kernel(place_ref, *refs):
    blocks, w_ref, own_ref, other_ref = refs[:9], refs[9], refs[10], refs[11]
    z, side = place_ref[0], place_ref[1]
    shifts = (0, -1, -2, -3, 1, 2, 3, 4)
    values = [b[...] for b in blocks[:7]]
    values.append(jnp.concatenate([blocks[7][...], blocks[8][...]], axis=0))
    for out_ref, half in ((own_ref, side), (other_ref, 1 - side)):
        total = None
        for shift, value in zip(shifts, values):
            row = lax.rem(z + shift + RING, RING)
            term = jnp.dot(value, w_ref[half * RING + row], preferred_element_type=F32)
            total = term if total is None else total + term
        out_ref[...] = total.astype(out_ref.dtype)


def local(streams, taps, residues, decay, skip, w_out):
    tokens, chans = streams.shape[1], streams.shape[2]
    chunk = tokens // CHUNKS
    tiles = chans // LANES
    ctx = lax.axis_index("ctx")
    ch = lax.axis_index("ch")

    halo = lax.ppermute(streams[:, tokens - 2 :, :], "ctx", [(i, i + 1) for i in range(CTX - 1)])
    swap = []
    for h in range(2):
        for a in range(RING):
            for y in range(2):
                for z in range(RING):
                    swap.append((((h * RING + a) * 2 + y) * RING + z, ((h * RING + z) * 2 + y) * RING + a))
    w_block = lax.ppermute(w_out, ("ctx", "ch"), swap)
    w_all = lax.all_gather(w_block, "ctx")

    decay_t, res_t = decay.T, residues.T
    skip_row = skip[None, :]
    me = jnp.reshape(ctx, (1,)).astype(jnp.int32)
    smem = pl.BlockSpec(memory_space=pltpu.SMEM)
    params = pltpu.CompilerParams(vmem_limit_bytes=VMEM_LIMIT)
    lane = lambda *lead: pl.BlockSpec((*lead, LANES), lambda g: (*([0] * len(lead)), g))

    drive, segend, start, send = pl.pallas_call(
        states_kernel,
        grid=(tiles,),
        in_specs=[
            smem,
            pl.BlockSpec((1, tokens, LANES), lambda g: (1, 0, g)),
            pl.BlockSpec((1, tokens, LANES), lambda g: (2, 0, g)),
            lane(3, 2),
            lane(3, 3),
            lane(MODES),
        ],
        out_specs=[lane(tokens), lane(CHUNKS, MODES, SEGS), lane(CHUNKS, MODES), lane(CTX, MODES)],
        out_shape=[
            jax.ShapeDtypeStruct((tokens, chans), F32),
            jax.ShapeDtypeStruct((CHUNKS, MODES, SEGS, chans), F32),
            jax.ShapeDtypeStruct((CHUNKS, MODES, chans), F32),
            jax.ShapeDtypeStruct((CTX, MODES, chans), F32),
        ],
        scratch_shapes=[
            pltpu.VMEM((tokens + 8, LANES), F32),
            pltpu.VMEM((tokens + 8, LANES), F32),
            pltpu.VMEM((CHUNKS, MODES, LANES), F32),
        ],
        compiler_params=params,
        name="states",
    )(me, streams, streams, halo, taps, decay_t)
    recv = lax.all_to_all(send, "ctx", 0, 0)

    def gate(c):
        if c == 0:
            before, before_spec = halo, lane(1, 2)
        else:
            before = streams
            before_spec = pl.BlockSpec((1, 16, LANES), lambda g: (0, c * chunk // 16 - 1, g))
        return pl.pallas_call(
            functools.partial(gate_kernel, c),
            grid=(tiles,),
            in_specs=[
                pl.BlockSpec((1, chunk, LANES), lambda g: (0, c, g)),
                before_spec,
                lane(3, 3),
                lane(MODES),
                lane(MODES),
                lane(1),
                pl.BlockSpec((chunk, LANES), lambda g: (c, g)),
                pl.BlockSpec((1, MODES, SEGS, LANES), lambda g: (c, 0, 0, g)),
                pl.BlockSpec((1, MODES, LANES), lambda g: (c, 0, g)),
                lane(CTX, MODES),
            ],
            out_specs=lane(chunk),
            out_shape=jax.ShapeDtypeStruct((chunk, chans), BF16),
            scratch_shapes=[pltpu.VMEM((chunk + 8, LANES), F32), pltpu.VMEM((chunk, LANES), F32)],
            compiler_params=params,
            name="gate",
        )(streams, before, taps, decay_t, res_t, skip_row, drive, segend, start, recv)

    up = [(y * RING + z, y * RING + (z + 1) % RING) for y in range(2) for z in range(RING)]
    down = [(d, s) for s, d in up]
    across = [(i, (i + RING) % CH) for i in range(CH)]
    half = chunk // 2
    place = jnp.stack([lax.rem(ch, RING), ch // RING]).astype(jnp.int32)

    gated = [gate(c) for c in range(CHUNKS)]
    held = [[g] for g in gated]
    from_low = list(gated)
    from_high = list(gated)
    lows = [[] for _ in range(CHUNKS)]
    highs = [[] for _ in range(CHUNKS)]
    for s in range(1, 5):
        for c in range(CHUNKS):
            a, b = from_low[c], from_high[c]
            if s == 4:
                a, b = a[:half], b[half:]
            from_low[c] = lax.ppermute(a, "ch", up)
            from_high[c] = lax.ppermute(b, "ch", down)
            lows[c].append(from_low[c])
            highs[c].append(from_high[c])

    outs = []
    for c in range(CHUNKS):
        parts = [gated[c], *lows[c][:3], *highs[c][:3], lows[c][3], highs[c][3]]
        own, other = pl.pallas_call(
            project_kernel,
            in_specs=[smem] + [pl.BlockSpec(memory_space=pltpu.VMEM)] * 10,
            out_specs=[pl.BlockSpec(memory_space=pltpu.VMEM)] * 2,
            out_shape=[
                jax.ShapeDtypeStruct((chunk, chans), F32),
                jax.ShapeDtypeStruct((chunk, chans), BF16),
            ],
            compiler_params=params,
            name="project",
        )(place, *parts, w_all)
        theirs = lax.ppermute(other, "ch", across)
        outs.append((own + theirs.astype(F32)).astype(BF16))
    return jnp.concatenate(outs, axis=0)


def solution(mesh):
    return jax.shard_map(
        local,
        mesh=mesh,
        in_specs=(
            P(None, "ctx", "ch"),
            P(None, None, "ch"),
            P("ch", None),
            P("ch", None),
            P("ch"),
            P("ch", "ctx"),
        ),
        out_specs=P("ctx", "ch"),
        check_vma=False,
    )
```

```python
import functools

import jax
import jax.numpy as jnp
from jax import lax
from jax.experimental import pallas as pl
from jax.experimental.pallas import tpu as pltpu
from jax.sharding import PartitionSpec as P

MODES = 16
LANES = 128
SEGS = 8
CHUNKS = ((0, 512), (512, 512), (1024, 512))
ROWS = 48
TILE = 256
CTX = 16
CH = 16
RING = 8
F32 = jnp.float32
BF16 = jnp.bfloat16
MIB = 1024 * 1024


PLAN = [
    ("hop", 0, 1),
    ("hop", 1, 1),
    ("later", 2, 0, 1),
    ("hop", 0, 2),
    ("hop", 2, 1),
    ("hop", 1, 2),
    ("hop", 0, 3),
    ("hop", 2, 2),
    ("hop", 1, 3),
    ("hop", 0, 4, "up"),
    ("hop", 2, 3),
    ("hop", 1, 4, "down"),
    ("hop", 2, 4),
    ("project", 0),
    ("project", 1),
    ("project", 2),
]


def row_ids():
    return lax.broadcasted_iota(jnp.int32, (SEGS, LANES), 0)


def wide(row):
    return jnp.broadcast_to(row, (SEGS, LANES))


def states_kernel(
    k_ref, v_ref, q_tail_ref, taps_ref, decay_ref, res_ref,
    drive_ref, segend_ref, start_ref, send_ref, modes_ref, kx, vx,
):
    tokens = k_ref.shape[1]
    kx[pl.ds(0, 8), :] = jnp.zeros((8, LANES), F32)
    vx[pl.ds(0, 8), :] = jnp.zeros((8, LANES), F32)
    kx[pl.ds(8, tokens), :] = k_ref[0].astype(F32)
    vx[pl.ds(8, tokens), :] = v_ref[0].astype(F32)
    decay = decay_ref[...]
    modes_ref[0] = decay
    modes_ref[1] = res_ref[...] * jnp.sqrt(decay)
    keep = jnp.exp(-decay)
    keeps = [wide(keep[m : m + 1]) for m in range(MODES)]
    tk = [wide(taps_ref[1, j : j + 1, :]) for j in range(3)]
    tv = [wide(taps_ref[2, j : j + 1, :]) for j in range(3)]
    later = (SEGS - 1 - row_ids()).astype(F32)
    state = jnp.zeros((MODES, LANES), F32)

    for c, (offset, chunk) in enumerate(CHUNKS):
        steps = chunk // SEGS

        def at(ref, i):
            return ref[pl.ds(8 + offset + i, SEGS, stride=steps), :]

        def step(i, carry):
            k1, k2, v1, v2, acc = carry
            k0, v0 = at(kx, i), at(vx, i)
            keyed = tk[0] * k0 + tk[1] * k1 + tk[2] * k2
            valued = tv[0] * v0 + tv[1] * v1 + tv[2] * v2
            drive = keyed * valued
            drive_ref[pl.ds(pl.multiple_of(offset + i * SEGS, SEGS), SEGS), :] = drive
            return k0, k1, v0, v1, tuple(a * s + drive for a, s in zip(keeps, acc))

        zero = tuple(jnp.zeros((SEGS, LANES), F32) for _ in range(MODES))
        acc = lax.fori_loop(
            0, steps, step,
            (at(kx, -1), at(kx, -2), at(vx, -1), at(vx, -2), zero),
            unroll=8,
        )[4]
        start_ref[c] = state
        ends = []
        for m in range(MODES):
            segend_ref[c, m] = acc[m]
            weight = jnp.exp(-wide(decay[m : m + 1]) * (later * steps))
            ends.append(jnp.sum(acc[m] * weight, axis=0, keepdims=True))
        state = state * jnp.exp(-decay * chunk) + jnp.concatenate(ends, axis=0)

    tail = q_tail_ref.shape[1] - 2
    upper = state.astype(BF16).astype(F32)
    payload = jnp.concatenate(
        [
            upper,
            state - upper,
            kx[pl.ds(8, 2), :],
            vx[pl.ds(8, 2), :],
            q_tail_ref[0].astype(F32)[tail:],
            kx[pl.ds(6 + tokens, 2), :],
            vx[pl.ds(6 + tokens, 2), :],
            jnp.zeros((ROWS - 2 * MODES - 10, LANES), F32),
        ],
        axis=0,
    ).astype(BF16)
    for j in range(CTX):
        send_ref[j] = payload


def first_drive(taps_ref, heads, tails):
    short, full = [], []
    for s in (1, 2):
        t0, t1, t2 = (taps_ref[s, j : j + 1, :] for j in range(3))
        (x0, x1), (p2, p1) = heads[s - 1], tails[s - 1]
        short.append((t0 * x0, t0 * x1 + t1 * x0))
        full.append((short[-1][0] + t1 * p1 + t2 * p2, short[-1][1] + t2 * p1))
    return [full[0][i] * full[1][i] - short[0][i] * short[1][i] for i in range(2)]


def incoming_states(me, tokens, taps_ref, decay, recv_ref):
    span = jnp.exp(-decay * tokens)
    near = jnp.exp(-decay * (tokens - 1))
    next_to_near = jnp.exp(-decay * (tokens - 2))
    state = jnp.zeros((MODES, LANES), F32)
    extra = [jnp.zeros((1, LANES), F32)] * 2
    q_halo = jnp.zeros((2, LANES), F32)
    raw = [recv_ref[i, pl.ds(2 * MODES, 16), :].astype(F32) for i in range(CTX)]
    for i in range(CTX):
        ended = recv_ref[i, :MODES, :].astype(F32) + recv_ref[i, MODES : 2 * MODES, :].astype(F32)
        if i > 0:
            heads = [[raw[i][r : r + 1], raw[i][r + 1 : r + 2]] for r in (0, 2)]
            tails = [[raw[i - 1][r : r + 1], raw[i - 1][r + 1 : r + 2]] for r in (6, 8)]
            d0, d1 = first_drive(taps_ref, heads, tails)
            extra = [jnp.where(me == i, d, e) for d, e in zip((d0, d1), extra)]
            q_halo = jnp.where(me == i, raw[i - 1][4:6], q_halo)
            ended = ended + near * d0 + next_to_near * d1
        state = jnp.where(i < me, state * span + ended, state)
    return state, extra, q_halo


def gate_kernel(group, tokens, *refs):
    first = group[0] == 0
    if first:
        (me_ref, q_ref, taps_ref, modes_ref, skip_ref, drive_ref, segend_ref, start_ref, recv_ref) = refs[:9]
        out_refs = refs[9 : 9 + len(group)]
        (entry_ref, qx, gx) = refs[9 + len(group) :]
    else:
        (q_ref, qb_ref, taps_ref, modes_ref, skip_ref, drive_ref, segend_ref, entry_ref) = refs[:8]
        out_refs = refs[8 : 8 + len(group)]
        (qx, gx) = refs[8 + len(group) :]
    decay = modes_ref[0]
    qx[pl.ds(8, q_ref.shape[1]), :] = q_ref[0].astype(F32)
    extra = None
    if first:
        state, extra, q_halo = incoming_states(me_ref[0], tokens, taps_ref, decay, recv_ref)
        qx[pl.ds(6, 2), :] = q_halo
        entries = [state]
        for c in range(1, len(CHUNKS)):
            offset = CHUNKS[c][0]
            entries.append(
                jnp.exp(-decay * offset) * state
                + start_ref[c]
                + jnp.exp(-decay * (offset - 1)) * extra[0]
                + jnp.exp(-decay * (offset - 2)) * extra[1]
            )
            if c not in group:
                entry_ref[c - len(group)] = entries[c]
    else:
        before = qb_ref[0].astype(F32)
        qx[pl.ds(6, 2), :] = before[before.shape[0] - 2 :]
        entries = [entry_ref[k] for k in range(len(group))]
    keep = jnp.exp(-decay)
    scaled = modes_ref[1]
    rows = row_ids()
    keeps = [wide(keep[m : m + 1]) for m in range(MODES)]
    gains = [wide(scaled[m : m + 1]) for m in range(MODES)]
    tq = [wide(taps_ref[0, j : j + 1, :]) for j in range(3)]
    skip = wide(skip_ref[...])

    for k, c in enumerate(group):
        offset, chunk = CHUNKS[c]
        base = offset - CHUNKS[group[0]][0]
        steps = chunk // SEGS
        keep1 = jnp.exp(-decay * steps)
        keep2 = jnp.exp(-decay * (2 * steps))
        keep4 = jnp.exp(-decay * (4 * steps))
        if c == 0:
            fix = jnp.exp(-decay * (steps - 1)) * extra[0] + jnp.exp(-decay * (steps - 2)) * extra[1]
        acc = []
        for m in range(MODES):
            ended = segend_ref[k, m]
            if c == 0:
                ended = ended + jnp.where(rows == 0, wide(fix[m : m + 1]), 0.0)
            x = jnp.where(rows == 0, wide(entries[k][m : m + 1]), pltpu.roll(ended, 1, 0))
            for far, factor in ((1, keep1), (2, keep2), (4, keep4)):
                moved = pltpu.roll(x, far, 0) * wide(factor[m : m + 1])
                x = x + jnp.where(rows >= far, moved, 0.0)
            acc.append(x)

        def at(i):
            return qx[pl.ds(8 + base + i, SEGS, stride=steps), :]

        def step(i, carry, more=None):
            q1, q2, acc = carry
            q0 = at(i)
            drive = drive_ref[pl.ds(pl.multiple_of(base + i * SEGS, SEGS), SEGS), :]
            if more is not None:
                drive = drive + jnp.where(rows == 0, wide(more), 0.0)
            acc = tuple(a * s + drive for a, s in zip(keeps, acc))
            terms = [g * s for g, s in zip(gains, acc)] + [skip * drive]
            while len(terms) > 1:
                terms = [sum(terms[i + 1 : i + 2], terms[i]) for i in range(0, len(terms), 2)]
            query = tq[0] * q0 + tq[1] * q1 + tq[2] * q2
            gx[pl.ds(base + i, SEGS, stride=steps), :] = query * terms[0]
            return q0, q1, acc

        carry = (at(-1), at(-2), tuple(acc))
        begin = 0
        if c == 0:
            for begin in range(4):
                carry = step(begin, carry, extra[begin] if begin < 2 else None)
            begin = 4
        lax.fori_loop(begin, steps, step, carry, unroll=4)
        out_refs[k][...] = gx[pl.ds(base, chunk), :].astype(BF16)


def project_kernel(side_ref, *refs):
    w_ref, own_ref, other_ref = refs[-3:]
    values = [r[...] for r in refs[:-3]]
    if len(values) == 9:
        far = jnp.where(pl.program_id(0) < pl.num_programs(0) // 2, values[4], values[5])
        values = values[:4] + [far] + values[6:]
    rows = jnp.concatenate(values, axis=1)
    side = side_ref[0]
    own_ref[...] = jnp.dot(rows, w_ref[side], preferred_element_type=F32)
    other_ref[...] = jnp.dot(rows, w_ref[1 - side], preferred_element_type=F32).astype(BF16)


def local(streams, taps, residues, decay, skip, w_out):
    tokens, chans = streams.shape[1], streams.shape[2]
    tiles = chans // LANES
    ctx = lax.axis_index("ctx")
    ch = lax.axis_index("ch")

    swap = []
    for h in range(2):
        for a in range(RING):
            for y in range(2):
                for z in range(RING):
                    there = h * RING + (z - a) % RING
                    swap.append((((h * RING + a) * 2 + y) * RING + z, (there * 2 + y) * RING + a))
    w_block = lax.ppermute(w_out, ("ctx", "ch"), swap)

    skip_row = skip[None, :]
    me = jnp.reshape(ctx, (1,)).astype(jnp.int32)
    smem = pl.BlockSpec(memory_space=pltpu.SMEM)
    cost = pl.CostEstimate(flops=4_000_000_000, bytes_accessed=4_000_000, transcendentals=0)
    params = lambda mib: pltpu.CompilerParams(vmem_limit_bytes=mib * MIB)
    lane = lambda *lead: pl.BlockSpec((*lead, LANES), lambda g: (*([0] * len(lead)), g))

    drive, segend, start, send, modes = pl.pallas_call(
        states_kernel,
        grid=(tiles,),
        in_specs=[
            pl.BlockSpec((1, tokens, LANES), lambda g: (1, 0, g)),
            pl.BlockSpec((1, tokens, LANES), lambda g: (2, 0, g)),
            pl.BlockSpec((1, 16, LANES), lambda g: (0, tokens // 16 - 1, g)),
            lane(3, 3),
            lane(MODES),
            lane(MODES),
        ],
        out_specs=[
            lane(tokens),
            lane(len(CHUNKS), MODES, SEGS),
            lane(len(CHUNKS), MODES),
            lane(CTX, ROWS),
            lane(2, MODES),
        ],
        out_shape=[
            jax.ShapeDtypeStruct((tokens, chans), F32),
            jax.ShapeDtypeStruct((len(CHUNKS), MODES, SEGS, chans), F32),
            jax.ShapeDtypeStruct((len(CHUNKS), MODES, chans), F32),
            jax.ShapeDtypeStruct((CTX, ROWS, chans), BF16),
            jax.ShapeDtypeStruct((2, MODES, chans), F32),
        ],
        scratch_shapes=[pltpu.VMEM((tokens + 8, LANES), F32)] * 2,
        compiler_params=params(60),
        cost_estimate=cost,
        name="states",
    )(streams, streams, streams, taps, decay.T, residues.T)
    w_block, send = lax.optimization_barrier((w_block, send))
    w_all = lax.all_gather(w_block, "ctx").reshape(2, RING * chans, w_out.shape[1])
    recv = lax.all_to_all(send, "ctx", 0, 0)

    def gate(group, entry):
        offset, size = CHUNKS[group[0]][0], sum(CHUNKS[c][1] for c in group)
        many, rest = len(group), len(CHUNKS) - len(group)
        q_spec = pl.BlockSpec((1, size, LANES), lambda g: (0, offset // size, g))
        shared_specs = [
            lane(3, 3),
            lane(2, MODES),
            lane(1),
            pl.BlockSpec((size, LANES), lambda g: (offset // size, g)),
            pl.BlockSpec((many, MODES, SEGS, LANES), lambda g: (group[0] // many, 0, 0, g)),
        ]
        shared = [taps, modes, skip_row, drive, segend]
        out_specs = [lane(CHUNKS[c][1]) for c in group]
        out_shape = [jax.ShapeDtypeStruct((CHUNKS[c][1], chans), BF16) for c in group]
        if group[0] == 0:
            in_specs = [smem, q_spec, *shared_specs, lane(len(CHUNKS), MODES), lane(CTX, ROWS)]
            args = [me, streams, *shared, start, recv]
            out_specs.append(lane(rest, MODES))
            out_shape.append(jax.ShapeDtypeStruct((rest, MODES, chans), F32))
        else:
            before = pl.BlockSpec((1, 16, LANES), lambda g: (0, offset // 16 - 1, g))
            in_specs = [q_spec, before, *shared_specs, lane(rest if many > rest else many, MODES)]
            args = [streams, streams, *shared, entry]
        return pl.pallas_call(
            functools.partial(gate_kernel, group, tokens),
            grid=(tiles,),
            in_specs=in_specs,
            out_specs=out_specs,
            out_shape=out_shape,
            scratch_shapes=[pltpu.VMEM((size + 8, LANES), F32), pltpu.VMEM((size, LANES), F32)],
            compiler_params=params(60),
            cost_estimate=cost,
            name="gate",
        )(*args)

    up = [(y * RING + z, y * RING + (z + 1) % RING) for y in range(2) for z in range(RING)]
    down = [(d, s) for s, d in up]
    across = [(i, (i + RING) % CH) for i in range(CH)]
    side = jnp.reshape(ch // RING, (1,)).astype(jnp.int32)

    *gated, entry = gate((0, 1), None)
    gated += gate((2,), entry)
    count = len(CHUNKS)
    low = [[g] for g in gated]
    high = [[g] for g in gated]

    def hop(c, s, *ways):
        a, b = low[c][-1], high[c][-1]
        if len(ways) == 0:
            ways = ("up", "down")
            if s == RING // 2:
                half = a.shape[0] // 2
                a, b = a[:half], b[half:]
        if "up" in ways:
            low[c].append(lax.ppermute(a, "ch", up))
        if "down" in ways:
            high[c].append(lax.ppermute(b, "ch", down))

    def later(d, c, s):
        low[c][s], high[c][s], g = lax.optimization_barrier((low[c][s], high[c][s], low[d][0]))
        low[d][0], high[d][0] = g, g

    def after(c, d):
        low[c][0], low[d][3], high[d][3] = lax.optimization_barrier((low[c][0], low[d][3], high[d][3]))

    tile = pl.BlockSpec((TILE, chans), lambda g: (g, 0))
    own = [None] * count
    theirs = [None] * count

    def project(c):
        chunk = CHUNKS[c][1]
        far = [*low[c][4:], *high[c][4:]]
        parts = [low[c][0], *high[c][1:4], *far, *low[c][3:0:-1]]
        count = chunk // TILE
        far_specs = [tile]
        if len(far) == 2:
            far_specs = [
                pl.BlockSpec((TILE, chans), lambda g: (jnp.minimum(g, count // 2 - 1), 0)),
                pl.BlockSpec((TILE, chans), lambda g: (jnp.maximum(g - count // 2, 0), 0)),
            ]
        mine, other = pl.pallas_call(
            project_kernel,
            grid=(count,),
            in_specs=[smem] + [tile] * 4 + far_specs + [tile] * 3 + [pl.BlockSpec(w_all.shape, lambda g: (0, 0, 0))],
            out_specs=[tile] * 2,
            out_shape=[
                jax.ShapeDtypeStruct((chunk, chans), F32),
                jax.ShapeDtypeStruct((chunk, chans), BF16),
            ],
            compiler_params=params(60),
            cost_estimate=cost,
            name="project",
        )(side, *parts, w_all)
        own[c] = mine
        theirs[c] = lax.ppermute(other, "ch", across)

    steps = {"hop": hop, "later": later, "after": after, "project": project}
    for kind, *rest in PLAN:
        steps[kind](*rest)

    outs = [(mine + other.astype(F32)).astype(BF16) for mine, other in zip(own, theirs)]
    return jnp.concatenate(outs, axis=0)


def solution(mesh):
    return jax.shard_map(
        local,
        mesh=mesh,
        in_specs=(
            P(None, "ctx", "ch"),
            P(None, None, "ch"),
            P("ch", None),
            P("ch", None),
            P("ch"),
            P("ch", "ctx"),
        ),
        out_specs=P("ctx", "ch"),
        check_vma=False,
    )
```

```python
import functools

import jax
import jax.numpy as jnp
from jax import lax
from jax.experimental import pallas as pl
from jax.experimental.pallas import tpu as pltpu
from jax.sharding import PartitionSpec as P

MODES = 16
LANES = 128
SEGS = 8
CHUNKS = ((0, 512), (512, 512), (1024, 512))
ROWS = 48
CTX = 16
CH = 16
RING = 8
F32 = jnp.float32
BF16 = jnp.bfloat16
MIB = 1024 * 1024


PLAN = (
    ("weights", 1, 0, "u"),
    ("hop", 0, 1, "ud"),
    ("hop", 1, 1, "ud"),
    ("hop", 0, 2, "ud"),
    ("wait", 2, 1, 0, 1),
    ("hop", 2, 1, "ud"),
    ("hop", 1, 2, "ud"),
    ("hop", 0, 3, "ud"),
    ("hop", 2, 2, "ud"),
    ("hop", 1, 3, "ud"),
    ("hop", 0, 4, "u"),
    ("hop", 2, 3, "ud"),
    ("hop", 1, 4, "d"),
    ("hop", 2, 4, "ud"),
    ("project", 0),
    ("project", 1),
    ("project", 2),
)


def row_ids():
    return lax.broadcasted_iota(jnp.int32, (SEGS, LANES), 0)


def wide(row):
    return jnp.broadcast_to(row, (SEGS, LANES))


def states_kernel(
    k_ref, v_ref, q_tail_ref, taps_ref, decay_ref, res_ref,
    drive_ref, segend_ref, start_ref, send_ref, modes_ref, kx, vx,
):
    tokens = k_ref.shape[1]
    kx[pl.ds(0, 8), :] = jnp.zeros((8, LANES), F32)
    vx[pl.ds(0, 8), :] = jnp.zeros((8, LANES), F32)
    kx[pl.ds(8, tokens), :] = k_ref[0].astype(F32)
    vx[pl.ds(8, tokens), :] = v_ref[0].astype(F32)
    decay = decay_ref[...]
    modes_ref[0] = decay
    modes_ref[1] = res_ref[...] * jnp.sqrt(decay)
    keep = jnp.exp(-decay)
    keeps = [wide(keep[m : m + 1]) for m in range(MODES)]
    tk = [wide(taps_ref[1, j : j + 1, :]) for j in range(3)]
    tv = [wide(taps_ref[2, j : j + 1, :]) for j in range(3)]
    later = (SEGS - 1 - row_ids()).astype(F32)
    state = jnp.zeros((MODES, LANES), F32)

    for c, (offset, chunk) in enumerate(CHUNKS):
        steps = chunk // SEGS

        def at(ref, i):
            return ref[pl.ds(8 + offset + i, SEGS, stride=steps), :]

        def step(i, carry):
            k1, k2, v1, v2, acc = carry
            k0, v0 = at(kx, i), at(vx, i)
            keyed = tk[0] * k0 + tk[1] * k1 + tk[2] * k2
            valued = tv[0] * v0 + tv[1] * v1 + tv[2] * v2
            drive = keyed * valued
            drive_ref[pl.ds(pl.multiple_of(offset + i * SEGS, SEGS), SEGS), :] = drive
            return k0, k1, v0, v1, tuple(a * s + drive for a, s in zip(keeps, acc))

        zero = tuple(jnp.zeros((SEGS, LANES), F32) for _ in range(MODES))
        acc = lax.fori_loop(
            0, steps, step,
            (at(kx, -1), at(kx, -2), at(vx, -1), at(vx, -2), zero),
            unroll=8,
        )[4]
        start_ref[c] = state
        ends = []
        for m in range(MODES):
            segend_ref[c, m] = acc[m]
            weight = jnp.exp(-wide(decay[m : m + 1]) * (later * steps))
            ends.append(jnp.sum(acc[m] * weight, axis=0, keepdims=True))
        state = state * jnp.exp(-decay * chunk) + jnp.concatenate(ends, axis=0)

    tail = q_tail_ref.shape[1] - 2
    upper = state.astype(BF16).astype(F32)
    payload = jnp.concatenate(
        [
            upper,
            state - upper,
            kx[pl.ds(8, 2), :],
            vx[pl.ds(8, 2), :],
            q_tail_ref[0].astype(F32)[tail:],
            kx[pl.ds(6 + tokens, 2), :],
            vx[pl.ds(6 + tokens, 2), :],
            jnp.zeros((ROWS - 2 * MODES - 10, LANES), F32),
        ],
        axis=0,
    ).astype(BF16)
    for j in range(CTX):
        send_ref[j] = payload


def first_drive(taps_ref, heads, tails):
    short, full = [], []
    for s in (1, 2):
        t0, t1, t2 = (taps_ref[s, j : j + 1, :] for j in range(3))
        (x0, x1), (p2, p1) = heads[s - 1], tails[s - 1]
        short.append((t0 * x0, t0 * x1 + t1 * x0))
        full.append((short[-1][0] + t1 * p1 + t2 * p2, short[-1][1] + t2 * p1))
    return [full[0][i] * full[1][i] - short[0][i] * short[1][i] for i in range(2)]


def incoming_states(me, tokens, taps_ref, decay, recv_ref):
    span = jnp.exp(-decay * tokens)
    near = jnp.exp(-decay * (tokens - 1))
    next_to_near = jnp.exp(-decay * (tokens - 2))
    state = jnp.zeros((MODES, LANES), F32)
    extra = [jnp.zeros((1, LANES), F32)] * 2
    q_halo = jnp.zeros((2, LANES), F32)
    raw = [recv_ref[i, pl.ds(2 * MODES, 16), :].astype(F32) for i in range(CTX)]
    for i in range(CTX):
        ended = recv_ref[i, :MODES, :].astype(F32) + recv_ref[i, MODES : 2 * MODES, :].astype(F32)
        if i > 0:
            heads = [[raw[i][r : r + 1], raw[i][r + 1 : r + 2]] for r in (0, 2)]
            tails = [[raw[i - 1][r : r + 1], raw[i - 1][r + 1 : r + 2]] for r in (6, 8)]
            d0, d1 = first_drive(taps_ref, heads, tails)
            extra = [jnp.where(me == i, d, e) for d, e in zip((d0, d1), extra)]
            q_halo = jnp.where(me == i, raw[i - 1][4:6], q_halo)
            ended = ended + near * d0 + next_to_near * d1
        state = jnp.where(i < me, state * span + ended, state)
    return state, extra, q_halo


def gate_kernel(group, tokens, *refs):
    first = group[0] == 0
    if first:
        (me_ref, q_ref, taps_ref, modes_ref, skip_ref, drive_ref, segend_ref, start_ref, recv_ref) = refs[:9]
        out_refs = refs[9 : 9 + len(group)]
        (entry_ref, qx, gx) = refs[9 + len(group) :]
    else:
        (q_ref, qb_ref, taps_ref, modes_ref, skip_ref, drive_ref, segend_ref, entry_ref) = refs[:8]
        out_refs = refs[8 : 8 + len(group)]
        (qx, gx) = refs[8 + len(group) :]
    decay = modes_ref[0]
    qx[pl.ds(8, q_ref.shape[1]), :] = q_ref[0].astype(F32)
    extra = None
    if first:
        state, extra, q_halo = incoming_states(me_ref[0], tokens, taps_ref, decay, recv_ref)
        qx[pl.ds(6, 2), :] = q_halo
        entries = [state]
        for c in range(1, len(CHUNKS)):
            offset = CHUNKS[c][0]
            entries.append(
                jnp.exp(-decay * offset) * state
                + start_ref[c]
                + jnp.exp(-decay * (offset - 1)) * extra[0]
                + jnp.exp(-decay * (offset - 2)) * extra[1]
            )
            if c not in group:
                entry_ref[c - len(group)] = entries[c]
    else:
        before = qb_ref[0].astype(F32)
        qx[pl.ds(6, 2), :] = before[before.shape[0] - 2 :]
        entries = [entry_ref[k] for k in range(len(group))]
    keep = jnp.exp(-decay)
    scaled = modes_ref[1]
    rows = row_ids()
    keeps = [wide(keep[m : m + 1]) for m in range(MODES)]
    gains = [wide(scaled[m : m + 1]) for m in range(MODES)]
    tq = [wide(taps_ref[0, j : j + 1, :]) for j in range(3)]
    skip = wide(skip_ref[...])

    for k, c in enumerate(group):
        offset, chunk = CHUNKS[c]
        base = offset - CHUNKS[group[0]][0]
        steps = chunk // SEGS
        keep1 = jnp.exp(-decay * steps)
        keep2 = jnp.exp(-decay * (2 * steps))
        keep4 = jnp.exp(-decay * (4 * steps))
        if c == 0:
            fix = jnp.exp(-decay * (steps - 1)) * extra[0] + jnp.exp(-decay * (steps - 2)) * extra[1]
        acc = []
        for m in range(MODES):
            ended = segend_ref[k, m]
            if c == 0:
                ended = ended + jnp.where(rows == 0, wide(fix[m : m + 1]), 0.0)
            x = jnp.where(rows == 0, wide(entries[k][m : m + 1]), pltpu.roll(ended, 1, 0))
            for far, factor in ((1, keep1), (2, keep2), (4, keep4)):
                moved = pltpu.roll(x, far, 0) * wide(factor[m : m + 1])
                x = x + jnp.where(rows >= far, moved, 0.0)
            acc.append(x)

        def at(i):
            return qx[pl.ds(8 + base + i, SEGS, stride=steps), :]

        def step(i, carry, more=None):
            q1, q2, acc = carry
            q0 = at(i)
            drive = drive_ref[pl.ds(pl.multiple_of(base + i * SEGS, SEGS), SEGS), :]
            if more is not None:
                drive = drive + jnp.where(rows == 0, wide(more), 0.0)
            acc = tuple(a * s + drive for a, s in zip(keeps, acc))
            terms = [g * s for g, s in zip(gains, acc)] + [skip * drive]
            while len(terms) > 1:
                terms = [sum(terms[i + 1 : i + 2], terms[i]) for i in range(0, len(terms), 2)]
            query = tq[0] * q0 + tq[1] * q1 + tq[2] * q2
            gx[pl.ds(base + i, SEGS, stride=steps), :] = query * terms[0]
            return q0, q1, acc

        carry = (at(-1), at(-2), tuple(acc))
        begin = 0
        if c == 0:
            for begin in range(4):
                carry = step(begin, carry, extra[begin] if begin < 2 else None)
            begin = 4
        lax.fori_loop(begin, steps, step, carry, unroll=4)
        out_refs[k][...] = gx[pl.ds(base, chunk), :].astype(BF16)


def project_kernel(place_ref, *refs):
    w_ref, own_ref, other_ref = refs[-3:]
    values = [r[...] for r in refs[:-3]]
    if len(values) == 9:
        far = jnp.where(pl.program_id(0) == 0, values[4], values[5])
        values = values[:4] + [far] + values[6:]
    rows = jnp.concatenate(values, axis=1)
    side = place_ref[0]
    own_ref[...] = jnp.dot(rows, w_ref[side], preferred_element_type=F32)
    other_ref[...] = jnp.dot(rows, w_ref[1 - side], preferred_element_type=F32).astype(BF16)


def local(streams, taps, residues, decay, skip, w_out):
    tokens, chans = streams.shape[1], streams.shape[2]
    tiles = chans // LANES
    ctx = lax.axis_index("ctx")
    ch = lax.axis_index("ch")

    swap = []
    for h in range(2):
        for a in range(RING):
            for y in range(2):
                for z in range(RING):
                    there = h * RING + (z - a) % RING
                    swap.append((((h * RING + a) * 2 + y) * RING + z, (there * 2 + y) * RING + a))

    skip_row = skip[None, :]
    me = jnp.reshape(ctx, (1,)).astype(jnp.int32)
    smem = pl.BlockSpec(memory_space=pltpu.SMEM)
    cost = pl.CostEstimate(flops=4_000_000_000, bytes_accessed=4_000_000, transcendentals=0)
    params = lambda mib: pltpu.CompilerParams(vmem_limit_bytes=mib * MIB)
    lane = lambda *lead: pl.BlockSpec((*lead, LANES), lambda g: (*([0] * len(lead)), g))

    drive, segend, start, send, modes = pl.pallas_call(
        states_kernel,
        grid=(tiles,),
        in_specs=[
            pl.BlockSpec((1, tokens, LANES), lambda g: (1, 0, g)),
            pl.BlockSpec((1, tokens, LANES), lambda g: (2, 0, g)),
            pl.BlockSpec((1, 16, LANES), lambda g: (0, tokens // 16 - 1, g)),
            lane(3, 3),
            lane(MODES),
            lane(MODES),
        ],
        out_specs=[
            lane(tokens),
            lane(len(CHUNKS), MODES, SEGS),
            lane(len(CHUNKS), MODES),
            lane(CTX, ROWS),
            lane(2, MODES),
        ],
        out_shape=[
            jax.ShapeDtypeStruct((tokens, chans), F32),
            jax.ShapeDtypeStruct((len(CHUNKS), MODES, SEGS, chans), F32),
            jax.ShapeDtypeStruct((len(CHUNKS), MODES, chans), F32),
            jax.ShapeDtypeStruct((CTX, ROWS, chans), BF16),
            jax.ShapeDtypeStruct((2, MODES, chans), F32),
        ],
        scratch_shapes=[pltpu.VMEM((tokens + 8, LANES), F32)] * 2,
        compiler_params=params(60),
        cost_estimate=cost,
        name="states",
    )(streams, streams, streams, taps, decay.T, residues.T)
    w_block, modes = lax.optimization_barrier((w_out, modes))
    w_block = lax.ppermute(w_block, ("ctx", "ch"), swap)
    recv = lax.all_to_all(send, "ctx", 0, 0)

    def gate(group, entry):
        offset, size = CHUNKS[group[0]][0], sum(CHUNKS[c][1] for c in group)
        many, rest = len(group), len(CHUNKS) - len(group)
        q_spec = pl.BlockSpec((1, size, LANES), lambda g: (0, offset // size, g))
        shared_specs = [
            lane(3, 3),
            lane(2, MODES),
            lane(1),
            pl.BlockSpec((size, LANES), lambda g: (offset // size, g)),
            pl.BlockSpec((many, MODES, SEGS, LANES), lambda g: (group[0] // many, 0, 0, g)),
        ]
        shared = [taps, modes, skip_row, drive, segend]
        out_specs = [lane(CHUNKS[c][1]) for c in group]
        out_shape = [jax.ShapeDtypeStruct((CHUNKS[c][1], chans), BF16) for c in group]
        if group[0] == 0:
            in_specs = [smem, q_spec, *shared_specs, lane(len(CHUNKS), MODES), lane(CTX, ROWS)]
            args = [me, streams, *shared, start, recv]
            out_specs.append(lane(rest, MODES))
            out_shape.append(jax.ShapeDtypeStruct((rest, MODES, chans), F32))
        else:
            before = pl.BlockSpec((1, 16, LANES), lambda g: (0, offset // 16 - 1, g))
            in_specs = [q_spec, before, *shared_specs, lane(rest if many > rest else many, MODES)]
            args = [streams, streams, *shared, entry]
        return pl.pallas_call(
            functools.partial(gate_kernel, group, tokens),
            grid=(tiles,),
            in_specs=in_specs,
            out_specs=out_specs,
            out_shape=out_shape,
            scratch_shapes=[pltpu.VMEM((size + 8, LANES), F32), pltpu.VMEM((size, LANES), F32)],
            compiler_params=params(60),
            cost_estimate=cost,
            name="gate",
        )(*args)

    up = [(y * RING + z, y * RING + (z + 1) % RING) for y in range(2) for z in range(RING)]
    down = [(d, s) for s, d in up]
    across = [(i, (i + RING) % CH) for i in range(CH)]
    place = jnp.reshape(ch // RING, (1,)).astype(jnp.int32)

    *gated, entry = gate((0, 1), None)
    gated += gate((2,), entry)
    count = len(CHUNKS)
    arrived = {(c, 0, way): g for c, g in enumerate(gated) for way in "ud"}

    def hop(c, s, ways):
        for way in ways:
            block = arrived[c, s - 1, way]
            if s == RING // 2 and len(ways) == 2:
                half = block.shape[0] // 2
                block = block[half:] if way == "u" else block[:half]
            arrived[c, s, way] = lax.ppermute(block, "ch", up if way == "u" else down)

    def wait(c, s, d, t):
        for way in "ud":
            if (d, t, way) in arrived and (c, s - 1, way) in arrived:
                pair = arrived[d, t, way], arrived[c, s - 1, way]
                arrived[d, t, way], arrived[c, s - 1, way] = lax.optimization_barrier(pair)

    own = [None] * count
    theirs = [None] * count

    def weights(c, s, way):
        nonlocal w_all
        w, arrived[c, s, way] = lax.optimization_barrier((w_block, arrived[c, s, way]))
        w_all = lax.all_to_all(jnp.broadcast_to(w, (CTX, *w.shape)), "ctx", 0, 0)
        w_all = w_all.reshape(2, RING * chans, w.shape[1])

    def project(c):
        chunk = CHUNKS[c][1]
        rows = chunk // 2
        get = lambda way, *hops: [arrived[c, s, way] for s in hops if (c, s, way) in arrived]
        parts = [gated[c], *get("d", 1, 2, 3, 4), *get("u", 4, 3, 2, 1)]
        far = len(parts) - 7
        tile = pl.BlockSpec((rows, chans), lambda g: (g, 0))
        whole = pl.BlockSpec((rows, chans), lambda g: (0, 0))
        mine, other = pl.pallas_call(
            project_kernel,
            grid=(2,),
            in_specs=[smem] + [tile] * 4 + [[tile], [whole] * 2][far - 1] + [tile] * 3 + [pl.BlockSpec(w_all.shape, lambda g: (0,) * w_all.ndim)],
            out_specs=[tile] * 2,
            out_shape=[
                jax.ShapeDtypeStruct((chunk, chans), F32),
                jax.ShapeDtypeStruct((chunk, chans), BF16),
            ],
            compiler_params=params(60),
            cost_estimate=cost,
            name="project",
        )(place, *parts, w_all)
        return mine, other

    def send(c, mine, other):
        own[c], theirs[c] = mine, lax.ppermute(other, "ch", across)

    def ahead(k, c, s):
        mine, other = project(k)
        block = [arrived[c, s - 1, way] for way in "ud"]
        other, block = lax.optimization_barrier((other, block))
        arrived[c, s - 1, "u"], arrived[c, s - 1, "d"] = block
        send(k, mine, other)

    w_all = None
    steps = {"weights": weights, "hop": hop, "wait": wait, "ahead": ahead, "project": lambda c: send(c, *project(c))}
    for kind, *rest in PLAN:
        steps[kind](*rest)

    outs = [(mine + other.astype(F32)).astype(BF16) for mine, other in zip(own, theirs)]
    return jnp.concatenate(outs, axis=0)


def solution(mesh):
    return jax.shard_map(
        local,
        mesh=mesh,
        in_specs=(
            P(None, "ctx", "ch"),
            P(None, None, "ch"),
            P("ch", None),
            P("ch", None),
            P("ch"),
            P("ch", "ctx"),
        ),
        out_specs=P("ctx", "ch"),
        check_vma=False,
    )
```

```python
import functools

import jax
import jax.numpy as jnp
from jax import lax
from jax.experimental import pallas as pl
from jax.experimental.pallas import tpu as pltpu
from jax.sharding import PartitionSpec as P

MODES = 16
LANES = 128
SEGS = 8
CHUNKS = ((0, 512), (512, 512), (1024, 512))
ROWS = 48
CTX = 16
CH = 16
RING = 8
F32 = jnp.float32
BF16 = jnp.bfloat16
MIB = 1024 * 1024


PLAN = (
    ("weights", 1, 0, "u"),
    ("hop", 0, 1, "ud"),
    ("hop", 1, 1, "ud"),
    ("hop", 0, 2, "ud"),
    ("wait", 2, 1, 0, 1),
    ("hop", 2, 1, "ud"),
    ("hop", 1, 2, "ud"),
    ("hop", 0, 3, "ud"),
    ("hop", 2, 2, "ud"),
    ("hop", 1, 3, "ud"),
    ("hop", 0, 4, "u"),
    ("hop", 2, 3, "ud"),
    ("hop", 1, 4, "d"),
    ("ahead", 0, 2, 4),
    ("hop", 2, 4, "ud"),
    ("project", 1),
    ("project", 2),
)


def row_ids():
    return lax.broadcasted_iota(jnp.int32, (SEGS, LANES), 0)


def wide(row):
    return jnp.broadcast_to(row, (SEGS, LANES))


def spread(ref, base, source, start, chunk):
    steps = chunk // SEGS
    for r in range(SEGS):
        at, row = base + r * (steps + 8), start + r * steps
        if row > 0:
            ref[pl.ds(at, steps + 8), :] = source[0, pl.ds(row - 16, steps + 16), :].astype(F32)[8:]
        else:
            ref[pl.ds(at + 8, steps), :] = source[0, pl.ds(0, steps), :].astype(F32)


def room(chunk):
    return chunk + SEGS * 8


def states_kernel(
    k_ref, v_ref, q_tail_ref, taps_ref, decay_ref, res_ref,
    drive_ref, segend_ref, start_ref, send_ref, modes_ref, kx, vx,
):
    tokens = k_ref.shape[1]
    kx[pl.ds(0, 8), :] = jnp.zeros((8, LANES), F32)
    vx[pl.ds(0, 8), :] = jnp.zeros((8, LANES), F32)
    decay = decay_ref[...]
    modes_ref[0] = decay
    modes_ref[1] = res_ref[...] * jnp.sqrt(decay)
    keep = jnp.exp(-decay)
    keeps = [wide(keep[m : m + 1]) for m in range(MODES)]
    tk = [wide(taps_ref[1, j : j + 1, :]) for j in range(3)]
    tv = [wide(taps_ref[2, j : j + 1, :]) for j in range(3)]
    later = (SEGS - 1 - row_ids()).astype(F32)
    state = jnp.zeros((MODES, LANES), F32)

    base = 0
    for c, (offset, chunk) in enumerate(CHUNKS):
        steps = chunk // SEGS
        spread(kx, base, k_ref, offset, chunk)
        spread(vx, base, v_ref, offset, chunk)

        def at(ref, i):
            return ref[pl.ds(base + 8 + i, SEGS, stride=steps + 8), :]

        def step(i, carry):
            k1, k2, v1, v2, acc = carry
            k0, v0 = at(kx, i), at(vx, i)
            keyed = tk[0] * k0 + tk[1] * k1 + tk[2] * k2
            valued = tv[0] * v0 + tv[1] * v1 + tv[2] * v2
            drive = keyed * valued
            drive_ref[pl.ds(pl.multiple_of(offset + i * SEGS, SEGS), SEGS), :] = drive
            return k0, k1, v0, v1, tuple(a * s + drive for a, s in zip(keeps, acc))

        zero = tuple(jnp.zeros((SEGS, LANES), F32) for _ in range(MODES))
        acc = lax.fori_loop(
            0, steps, step,
            (at(kx, -1), at(kx, -2), at(vx, -1), at(vx, -2), zero),
            unroll=16,
        )[4]
        start_ref[c] = state
        ends = []
        for m in range(MODES):
            segend_ref[c, m] = acc[m]
            weight = jnp.exp(-wide(decay[m : m + 1]) * (later * steps))
            ends.append(jnp.sum(acc[m] * weight, axis=0, keepdims=True))
        state = state * jnp.exp(-decay * chunk) + jnp.concatenate(ends, axis=0)
        base += room(chunk)

    tail = q_tail_ref.shape[1] - 2
    upper = state.astype(BF16).astype(F32)
    payload = jnp.concatenate(
        [
            upper,
            state - upper,
            kx[pl.ds(8, 2), :],
            vx[pl.ds(8, 2), :],
            q_tail_ref[0].astype(F32)[tail:],
            kx[pl.ds(base - 2, 2), :],
            vx[pl.ds(base - 2, 2), :],
            jnp.zeros((ROWS - 2 * MODES - 10, LANES), F32),
        ],
        axis=0,
    ).astype(BF16)
    for j in range(CTX):
        send_ref[j] = payload


def first_drive(taps_ref, heads, tails):
    short, full = [], []
    for s in (1, 2):
        t0, t1, t2 = (taps_ref[s, j : j + 1, :] for j in range(3))
        (x0, x1), (p2, p1) = heads[s - 1], tails[s - 1]
        short.append((t0 * x0, t0 * x1 + t1 * x0))
        full.append((short[-1][0] + t1 * p1 + t2 * p2, short[-1][1] + t2 * p1))
    return [full[0][i] * full[1][i] - short[0][i] * short[1][i] for i in range(2)]


def incoming_states(me, tokens, taps_ref, decay, recv_ref):
    span = jnp.exp(-decay * tokens)
    near = jnp.exp(-decay * (tokens - 1))
    next_to_near = jnp.exp(-decay * (tokens - 2))
    state = jnp.zeros((MODES, LANES), F32)
    extra = [jnp.zeros((1, LANES), F32)] * 2
    q_halo = jnp.zeros((2, LANES), F32)
    raw = [recv_ref[i, pl.ds(2 * MODES, 16), :].astype(F32) for i in range(CTX)]
    for i in range(CTX):
        ended = recv_ref[i, :MODES, :].astype(F32) + recv_ref[i, MODES : 2 * MODES, :].astype(F32)
        if i > 0:
            heads = [[raw[i][r : r + 1], raw[i][r + 1 : r + 2]] for r in (0, 2)]
            tails = [[raw[i - 1][r : r + 1], raw[i - 1][r + 1 : r + 2]] for r in (6, 8)]
            d0, d1 = first_drive(taps_ref, heads, tails)
            extra = [jnp.where(me == i, d, e) for d, e in zip((d0, d1), extra)]
            q_halo = jnp.where(me == i, raw[i - 1][4:6], q_halo)
            ended = ended + near * d0 + next_to_near * d1
        state = jnp.where(i < me, state * span + ended, state)
    return state, extra, q_halo


def gate_kernel(group, tokens, *refs):
    first = group[0] == 0
    if first:
        (me_ref, q_ref, taps_ref, modes_ref, skip_ref, drive_ref, segend_ref, start_ref, recv_ref) = refs[:9]
        out_refs = refs[9 : 9 + len(group)]
        (entry_ref, qx, gx) = refs[9 + len(group) :]
    else:
        (q_ref, qb_ref, taps_ref, modes_ref, skip_ref, drive_ref, segend_ref, entry_ref) = refs[:8]
        out_refs = refs[8 : 8 + len(group)]
        (qx, gx) = refs[8 + len(group) :]
    decay = modes_ref[0]
    extra = None
    if first:
        state, extra, q_halo = incoming_states(me_ref[0], tokens, taps_ref, decay, recv_ref)
        qx[pl.ds(6, 2), :] = q_halo
        entries = [state]
        for c in range(1, len(CHUNKS)):
            offset = CHUNKS[c][0]
            entries.append(
                jnp.exp(-decay * offset) * state
                + start_ref[c]
                + jnp.exp(-decay * (offset - 1)) * extra[0]
                + jnp.exp(-decay * (offset - 2)) * extra[1]
            )
            if c not in group:
                entry_ref[c - len(group)] = entries[c]
    else:
        before = qb_ref[0].astype(F32)
        qx[pl.ds(6, 2), :] = before[before.shape[0] - 2 :]
        entries = [entry_ref[k] for k in range(len(group))]
    keep = jnp.exp(-decay)
    scaled = modes_ref[1]
    rows = row_ids()
    keeps = [wide(keep[m : m + 1]) for m in range(MODES)]
    gains = [wide(scaled[m : m + 1]) for m in range(MODES)]
    tq = [wide(taps_ref[0, j : j + 1, :]) for j in range(3)]
    skip = wide(skip_ref[...])

    place = 0
    for k, c in enumerate(group):
        offset, chunk = CHUNKS[c]
        base = offset - CHUNKS[group[0]][0]
        steps = chunk // SEGS
        spread(qx, place, q_ref, base, chunk)
        keep1 = jnp.exp(-decay * steps)
        keep2 = jnp.exp(-decay * (2 * steps))
        keep4 = jnp.exp(-decay * (4 * steps))
        if c == 0:
            fix = jnp.exp(-decay * (steps - 1)) * extra[0] + jnp.exp(-decay * (steps - 2)) * extra[1]
        acc = []
        for m in range(MODES):
            ended = segend_ref[k, m]
            if c == 0:
                ended = ended + jnp.where(rows == 0, wide(fix[m : m + 1]), 0.0)
            x = jnp.where(rows == 0, wide(entries[k][m : m + 1]), pltpu.roll(ended, 1, 0))
            for far, factor in ((1, keep1), (2, keep2), (4, keep4)):
                moved = pltpu.roll(x, far, 0) * wide(factor[m : m + 1])
                x = x + jnp.where(rows >= far, moved, 0.0)
            acc.append(x)

        def at(i):
            return qx[pl.ds(place + 8 + i, SEGS, stride=steps + 8), :]

        def step(i, carry, more=None):
            q1, q2, acc = carry
            q0 = at(i)
            drive = drive_ref[pl.ds(pl.multiple_of(base + i * SEGS, SEGS), SEGS), :]
            if more is not None:
                drive = drive + jnp.where(rows == 0, wide(more), 0.0)
            acc = tuple(a * s + drive for a, s in zip(keeps, acc))
            terms = [g * s for g, s in zip(gains, acc)] + [skip * drive]
            while len(terms) > 1:
                terms = [sum(terms[i + 1 : i + 2], terms[i]) for i in range(0, len(terms), 2)]
            query = tq[0] * q0 + tq[1] * q1 + tq[2] * q2
            gx[pl.ds(place + i, SEGS, stride=steps + 8), :] = query * terms[0]
            return q0, q1, acc

        carry = (at(-1), at(-2), tuple(acc))
        begin = 0
        if c == 0:
            for begin in range(8):
                carry = step(begin, carry, extra[begin] if begin < 2 else None)
            begin = 8
        lax.fori_loop(begin, steps, step, carry, unroll=8)
        for r in range(SEGS):
            out_refs[k][pl.ds(r * steps, steps), :] = gx[pl.ds(place + r * (steps + 8), steps), :].astype(BF16)
        place += room(chunk)


def project_kernel(place_ref, *refs):
    w_ref, own_ref, other_ref = refs[-3:]
    values = [r[...] for r in refs[:-3]]
    if len(values) == 9:
        far = jnp.where(pl.program_id(0) == 0, values[4], values[5])
        values = values[:4] + [far] + values[6:]
    rows = jnp.concatenate(values, axis=1)
    side = place_ref[0]
    own_ref[...] = jnp.dot(rows, w_ref[side], preferred_element_type=F32)
    other_ref[...] = jnp.dot(rows, w_ref[1 - side], preferred_element_type=F32).astype(BF16)


def local(streams, taps, residues, decay, skip, w_out):
    tokens, chans = streams.shape[1], streams.shape[2]
    tiles = chans // LANES
    ctx = lax.axis_index("ctx")
    ch = lax.axis_index("ch")

    swap = []
    for h in range(2):
        for a in range(RING):
            for y in range(2):
                for z in range(RING):
                    there = h * RING + (z - a) % RING
                    swap.append((((h * RING + a) * 2 + y) * RING + z, (there * 2 + y) * RING + a))

    skip_row = skip[None, :]
    me = jnp.reshape(ctx, (1,)).astype(jnp.int32)
    smem = pl.BlockSpec(memory_space=pltpu.SMEM)
    cost = pl.CostEstimate(flops=4_000_000_000, bytes_accessed=4_000_000, transcendentals=0)
    params = lambda mib: pltpu.CompilerParams(vmem_limit_bytes=mib * MIB)
    lane = lambda *lead: pl.BlockSpec((*lead, LANES), lambda g: (*([0] * len(lead)), g))

    drive, segend, start, send, modes = pl.pallas_call(
        states_kernel,
        grid=(tiles,),
        in_specs=[
            pl.BlockSpec((1, tokens, LANES), lambda g: (1, 0, g)),
            pl.BlockSpec((1, tokens, LANES), lambda g: (2, 0, g)),
            pl.BlockSpec((1, 16, LANES), lambda g: (0, tokens // 16 - 1, g)),
            lane(3, 3),
            lane(MODES),
            lane(MODES),
        ],
        out_specs=[
            lane(tokens),
            lane(len(CHUNKS), MODES, SEGS),
            lane(len(CHUNKS), MODES),
            lane(CTX, ROWS),
            lane(2, MODES),
        ],
        out_shape=[
            jax.ShapeDtypeStruct((tokens, chans), F32),
            jax.ShapeDtypeStruct((len(CHUNKS), MODES, SEGS, chans), F32),
            jax.ShapeDtypeStruct((len(CHUNKS), MODES, chans), F32),
            jax.ShapeDtypeStruct((CTX, ROWS, chans), BF16),
            jax.ShapeDtypeStruct((2, MODES, chans), F32),
        ],
        scratch_shapes=[pltpu.VMEM((sum(room(n) for _, n in CHUNKS), LANES), F32)] * 2,
        compiler_params=params(60),
        cost_estimate=cost,
        name="states",
    )(streams, streams, streams, taps, decay.T, residues.T)
    w_block, modes = lax.optimization_barrier((w_out, modes))
    w_block = lax.ppermute(w_block, ("ctx", "ch"), swap)
    recv = lax.all_to_all(send, "ctx", 0, 0)

    def gate(group, entry):
        offset, size = CHUNKS[group[0]][0], sum(CHUNKS[c][1] for c in group)
        many, rest = len(group), len(CHUNKS) - len(group)
        q_spec = pl.BlockSpec((1, size, LANES), lambda g: (0, offset // size, g))
        shared_specs = [
            lane(3, 3),
            lane(2, MODES),
            lane(1),
            pl.BlockSpec((size, LANES), lambda g: (offset // size, g)),
            pl.BlockSpec((many, MODES, SEGS, LANES), lambda g: (group[0] // many, 0, 0, g)),
        ]
        shared = [taps, modes, skip_row, drive, segend]
        out_specs = [lane(CHUNKS[c][1]) for c in group]
        out_shape = [jax.ShapeDtypeStruct((CHUNKS[c][1], chans), BF16) for c in group]
        if group[0] == 0:
            in_specs = [smem, q_spec, *shared_specs, lane(len(CHUNKS), MODES), lane(CTX, ROWS)]
            args = [me, streams, *shared, start, recv]
            out_specs.append(lane(rest, MODES))
            out_shape.append(jax.ShapeDtypeStruct((rest, MODES, chans), F32))
        else:
            before = pl.BlockSpec((1, 16, LANES), lambda g: (0, offset // 16 - 1, g))
            in_specs = [q_spec, before, *shared_specs, lane(rest if many > rest else many, MODES)]
            args = [streams, streams, *shared, entry]
        return pl.pallas_call(
            functools.partial(gate_kernel, group, tokens),
            grid=(tiles,),
            in_specs=in_specs,
            out_specs=out_specs,
            out_shape=out_shape,
            scratch_shapes=[pltpu.VMEM((sum(room(CHUNKS[c][1]) for c in group), LANES), F32)] * 2,
            compiler_params=params(60),
            cost_estimate=cost,
            name="gate",
        )(*args)

    up = [(y * RING + z, y * RING + (z + 1) % RING) for y in range(2) for z in range(RING)]
    down = [(d, s) for s, d in up]
    across = [(i, (i + RING) % CH) for i in range(CH)]
    place = jnp.reshape(ch // RING, (1,)).astype(jnp.int32)

    *gated, entry = gate((0, 1), None)
    gated += gate((2,), entry)
    count = len(CHUNKS)
    arrived = {(c, 0, way): g for c, g in enumerate(gated) for way in "ud"}

    def hop(c, s, ways):
        for way in ways:
            block = arrived[c, s - 1, way]
            if s == RING // 2 and len(ways) == 2:
                half = block.shape[0] // 2
                block = block[half:] if way == "u" else block[:half]
            arrived[c, s, way] = lax.ppermute(block, "ch", up if way == "u" else down)

    def wait(c, s, d, t):
        for way in "ud":
            if (d, t, way) in arrived and (c, s - 1, way) in arrived:
                pair = arrived[d, t, way], arrived[c, s - 1, way]
                arrived[d, t, way], arrived[c, s - 1, way] = lax.optimization_barrier(pair)

    own = [None] * count
    theirs = [None] * count

    def weights(c, s, way):
        nonlocal w_all
        w, arrived[c, s, way] = lax.optimization_barrier((w_block, arrived[c, s, way]))
        w_all = lax.all_to_all(jnp.broadcast_to(w, (CTX, *w.shape)), "ctx", 0, 0)
        w_all = w_all.reshape(2, RING * chans, w.shape[1])

    def project(c):
        chunk = CHUNKS[c][1]
        rows = chunk // 2
        get = lambda way, *hops: [arrived[c, s, way] for s in hops if (c, s, way) in arrived]
        parts = [gated[c], *get("d", 1, 2, 3, 4), *get("u", 4, 3, 2, 1)]
        far = len(parts) - 7
        tile = pl.BlockSpec((rows, chans), lambda g: (g, 0))
        whole = pl.BlockSpec((rows, chans), lambda g: (0, 0))
        mine, other = pl.pallas_call(
            project_kernel,
            grid=(2,),
            in_specs=[smem] + [tile] * 4 + [[tile], [whole] * 2][far - 1] + [tile] * 3 + [pl.BlockSpec(w_all.shape, lambda g: (0,) * w_all.ndim)],
            out_specs=[tile] * 2,
            out_shape=[
                jax.ShapeDtypeStruct((chunk, chans), F32),
                jax.ShapeDtypeStruct((chunk, chans), BF16),
            ],
            compiler_params=params(20),
            cost_estimate=cost,
            name="project",
        )(place, *parts, w_all)
        return mine, other

    def send(c, mine, other):
        own[c], theirs[c] = mine, lax.ppermute(other, "ch", across)

    def ahead(k, c, s):
        mine, other = project(k)
        block = [arrived[c, s - 1, way] for way in "ud"]
        other, block = lax.optimization_barrier((other, block))
        arrived[c, s - 1, "u"], arrived[c, s - 1, "d"] = block
        send(k, mine, other)

    w_all = None
    steps = {"weights": weights, "hop": hop, "wait": wait, "ahead": ahead, "project": lambda c: send(c, *project(c))}
    for kind, *rest in PLAN:
        steps[kind](*rest)

    outs = [(mine + other.astype(F32)).astype(BF16) for mine, other in zip(own, theirs)]
    return jnp.concatenate(outs, axis=0)


def solution(mesh):
    return jax.shard_map(
        local,
        mesh=mesh,
        in_specs=(
            P(None, "ctx", "ch"),
            P(None, None, "ch"),
            P("ch", None),
            P("ch", None),
            P("ch"),
            P("ch", "ctx"),
        ),
        out_specs=P("ctx", "ch"),
        check_vma=False,
    )
```

```python
import functools

import jax
import jax.numpy as jnp
from jax import lax
from jax.experimental import pallas as pl
from jax.experimental.pallas import tpu as pltpu
from jax.sharding import PartitionSpec as P

MODES = 16
LANES = 128
SEGS = 8
CHUNKS = ((0, 512), (512, 512), (1024, 512))
ROWS = 48
CTX = 16
CH = 16
RING = 8
F32 = jnp.float32
BF16 = jnp.bfloat16
MIB = 1024 * 1024


PLAN = (
    ("weights", 1, 0, "u"),
    ("hop", 0, 1, "ud"),
    ("hop", 1, 1, "ud"),
    ("hop", 0, 2, "ud"),
    ("hop", 2, 1, "ud"),
    ("hop", 1, 2, "ud"),
    ("hop", 0, 3, "ud"),
    ("hop", 2, 2, "ud"),
    ("hop", 1, 3, "ud"),
    ("hop", 0, 4, "u"),
    ("hop", 2, 3, "ud"),
    ("hop", 1, 4, "d"),
    ("ahead", 0, 2, 4),
    ("hop", 2, 4, "ud"),
    ("project", 1),
    ("project", 2),
)


def row_ids():
    return lax.broadcasted_iota(jnp.int32, (SEGS, LANES), 0)


def wide(row):
    return jnp.broadcast_to(row, (SEGS, LANES))


def spread(ref, base, source, start, chunk):
    steps = chunk // SEGS
    for r in range(SEGS):
        at, row = base + r * (steps + 8), start + r * steps
        if row > 0:
            ref[pl.ds(at, steps + 8), :] = source[0, pl.ds(row - 16, steps + 16), :].astype(F32)[8:]
        else:
            ref[pl.ds(at + 8, steps), :] = source[0, pl.ds(0, steps), :].astype(F32)


def room(chunk):
    return chunk + SEGS * 8


def states_kernel(
    k_ref, v_ref, q_tail_ref, taps_ref, decay_ref, res_ref,
    drive_ref, segend_ref, start_ref, send_ref, modes_ref, kx, vx,
):
    tokens = k_ref.shape[1]
    kx[pl.ds(0, 8), :] = jnp.zeros((8, LANES), F32)
    vx[pl.ds(0, 8), :] = jnp.zeros((8, LANES), F32)
    decay = decay_ref[...]
    modes_ref[0] = decay
    modes_ref[1] = res_ref[...] * jnp.sqrt(decay)
    keep = jnp.exp(-decay)
    keeps = [wide(keep[m : m + 1]) for m in range(MODES)]
    tk = [wide(taps_ref[1, j : j + 1, :]) for j in range(3)]
    tv = [wide(taps_ref[2, j : j + 1, :]) for j in range(3)]
    later = (SEGS - 1 - row_ids()).astype(F32)
    state = jnp.zeros((MODES, LANES), F32)

    base = 0
    for c, (offset, chunk) in enumerate(CHUNKS):
        steps = chunk // SEGS
        spread(kx, base, k_ref, offset, chunk)
        spread(vx, base, v_ref, offset, chunk)

        def at(ref, i):
            return ref[pl.ds(base + 8 + i, SEGS, stride=steps + 8), :]

        def step(i, carry):
            k1, k2, v1, v2, acc = carry
            k0, v0 = at(kx, i), at(vx, i)
            keyed = tk[0] * k0 + tk[1] * k1 + tk[2] * k2
            valued = tv[0] * v0 + tv[1] * v1 + tv[2] * v2
            drive = keyed * valued
            drive_ref[pl.ds(pl.multiple_of(offset + i * SEGS, SEGS), SEGS), :] = drive
            return k0, k1, v0, v1, tuple(a * s + drive for a, s in zip(keeps, acc))

        zero = tuple(jnp.zeros((SEGS, LANES), F32) for _ in range(MODES))
        acc = lax.fori_loop(
            0, steps, step,
            (at(kx, -1), at(kx, -2), at(vx, -1), at(vx, -2), zero),
            unroll=16,
        )[4]
        start_ref[c] = state
        ends = []
        for m in range(MODES):
            segend_ref[c, m] = acc[m]
            weight = jnp.exp(-wide(decay[m : m + 1]) * (later * steps))
            ends.append(jnp.sum(acc[m] * weight, axis=0, keepdims=True))
        state = state * jnp.exp(-decay * chunk) + jnp.concatenate(ends, axis=0)
        base += room(chunk)

    tail = q_tail_ref.shape[1] - 2
    upper = state.astype(BF16).astype(F32)
    payload = jnp.concatenate(
        [
            upper,
            state - upper,
            kx[pl.ds(8, 2), :],
            vx[pl.ds(8, 2), :],
            q_tail_ref[0].astype(F32)[tail:],
            kx[pl.ds(base - 2, 2), :],
            vx[pl.ds(base - 2, 2), :],
            jnp.zeros((ROWS - 2 * MODES - 10, LANES), F32),
        ],
        axis=0,
    ).astype(BF16)
    for j in range(CTX):
        send_ref[j] = payload


def first_drive(taps_ref, heads, tails):
    short, full = [], []
    for s in (1, 2):
        t0, t1, t2 = (taps_ref[s, j : j + 1, :] for j in range(3))
        (x0, x1), (p2, p1) = heads[s - 1], tails[s - 1]
        short.append((t0 * x0, t0 * x1 + t1 * x0))
        full.append((short[-1][0] + t1 * p1 + t2 * p2, short[-1][1] + t2 * p1))
    return [full[0][i] * full[1][i] - short[0][i] * short[1][i] for i in range(2)]


def incoming_states(me, tokens, taps_ref, decay, recv_ref):
    span = jnp.exp(-decay * tokens)
    near = jnp.exp(-decay * (tokens - 1))
    next_to_near = jnp.exp(-decay * (tokens - 2))
    state = jnp.zeros((MODES, LANES), F32)
    extra = [jnp.zeros((1, LANES), F32)] * 2
    q_halo = jnp.zeros((2, LANES), F32)
    raw = [recv_ref[i, pl.ds(2 * MODES, 16), :].astype(F32) for i in range(CTX)]
    for i in range(CTX):
        ended = recv_ref[i, :MODES, :].astype(F32) + recv_ref[i, MODES : 2 * MODES, :].astype(F32)
        if i > 0:
            heads = [[raw[i][r : r + 1], raw[i][r + 1 : r + 2]] for r in (0, 2)]
            tails = [[raw[i - 1][r : r + 1], raw[i - 1][r + 1 : r + 2]] for r in (6, 8)]
            d0, d1 = first_drive(taps_ref, heads, tails)
            extra = [jnp.where(me == i, d, e) for d, e in zip((d0, d1), extra)]
            q_halo = jnp.where(me == i, raw[i - 1][4:6], q_halo)
            ended = ended + near * d0 + next_to_near * d1
        state = jnp.where(i < me, state * span + ended, state)
    return state, extra, q_halo


def gate_kernel(group, tokens, *refs):
    first = group[0] == 0
    if first:
        (me_ref, q_ref, taps_ref, modes_ref, skip_ref, drive_ref, segend_ref, start_ref, recv_ref) = refs[:9]
        out_refs = refs[9 : 9 + len(group)]
        (entry_ref, qx, gx) = refs[9 + len(group) :]
    else:
        (q_ref, qb_ref, taps_ref, modes_ref, skip_ref, drive_ref, segend_ref, entry_ref) = refs[:8]
        out_refs = refs[8 : 8 + len(group)]
        (qx, gx) = refs[8 + len(group) :]
    decay = modes_ref[0]
    extra = None
    if first:
        state, extra, q_halo = incoming_states(me_ref[0], tokens, taps_ref, decay, recv_ref)
        qx[pl.ds(6, 2), :] = q_halo
        entries = [state]
        for c in range(1, len(CHUNKS)):
            offset = CHUNKS[c][0]
            entries.append(
                jnp.exp(-decay * offset) * state
                + start_ref[c]
                + jnp.exp(-decay * (offset - 1)) * extra[0]
                + jnp.exp(-decay * (offset - 2)) * extra[1]
            )
            if c not in group:
                entry_ref[c - len(group)] = entries[c]
    else:
        before = qb_ref[0].astype(F32)
        qx[pl.ds(6, 2), :] = before[before.shape[0] - 2 :]
        entries = [entry_ref[k] for k in range(len(group))]
    keep = jnp.exp(-decay)
    scaled = modes_ref[1]
    rows = row_ids()
    keeps = [wide(keep[m : m + 1]) for m in range(MODES)]
    gains = [wide(scaled[m : m + 1]) for m in range(MODES)]
    tq = [wide(taps_ref[0, j : j + 1, :]) for j in range(3)]
    skip = wide(skip_ref[...])

    place = 0
    for k, c in enumerate(group):
        offset, chunk = CHUNKS[c]
        base = offset - CHUNKS[group[0]][0]
        steps = chunk // SEGS
        spread(qx, place, q_ref, base, chunk)
        keep1 = jnp.exp(-decay * steps)
        keep2 = jnp.exp(-decay * (2 * steps))
        keep4 = jnp.exp(-decay * (4 * steps))
        if c == 0:
            fix = jnp.exp(-decay * (steps - 1)) * extra[0] + jnp.exp(-decay * (steps - 2)) * extra[1]
        acc = []
        for m in range(MODES):
            ended = segend_ref[k, m]
            if c == 0:
                ended = ended + jnp.where(rows == 0, wide(fix[m : m + 1]), 0.0)
            x = jnp.where(rows == 0, wide(entries[k][m : m + 1]), pltpu.roll(ended, 1, 0))
            for far, factor in ((1, keep1), (2, keep2), (4, keep4)):
                moved = pltpu.roll(x, far, 0) * wide(factor[m : m + 1])
                x = x + jnp.where(rows >= far, moved, 0.0)
            acc.append(x)

        def at(i):
            return qx[pl.ds(place + 8 + i, SEGS, stride=steps + 8), :]

        def step(i, carry, more=None):
            q1, q2, acc = carry
            q0 = at(i)
            drive = drive_ref[pl.ds(pl.multiple_of(base + i * SEGS, SEGS), SEGS), :]
            if more is not None:
                drive = drive + jnp.where(rows == 0, wide(more), 0.0)
            acc = tuple(a * s + drive for a, s in zip(keeps, acc))
            terms = [g * s for g, s in zip(gains, acc)] + [skip * drive]
            while len(terms) > 1:
                terms = [sum(terms[i + 1 : i + 2], terms[i]) for i in range(0, len(terms), 2)]
            query = tq[0] * q0 + tq[1] * q1 + tq[2] * q2
            gx[pl.ds(place + i, SEGS, stride=steps + 8), :] = query * terms[0]
            return q0, q1, acc

        carry = (at(-1), at(-2), tuple(acc))
        begin = 0
        if c == 0:
            for begin in range(8):
                carry = step(begin, carry, extra[begin] if begin < 2 else None)
            begin = 8
        lax.fori_loop(begin, steps, step, carry, unroll=8)
        for r in range(SEGS):
            out_refs[k][pl.ds(r * steps, steps), :] = gx[pl.ds(place + r * (steps + 8), steps), :].astype(BF16)
        place += room(chunk)


def project_kernel(place_ref, *refs):
    w_ref, own_ref, other_ref = refs[-3:]
    values = [r[...] for r in refs[:-3]]
    if len(values) == 9:
        far = jnp.where(pl.program_id(0) == 0, values[4], values[5])
        values = values[:4] + [far] + values[6:]
    rows = jnp.concatenate(values, axis=1)
    side = place_ref[0]
    own_ref[...] = jnp.dot(rows, w_ref[side], preferred_element_type=F32)
    other_ref[...] = jnp.dot(rows, w_ref[1 - side], preferred_element_type=F32).astype(BF16)


def local(streams, taps, residues, decay, skip, w_out):
    tokens, chans = streams.shape[1], streams.shape[2]
    tiles = chans // LANES
    ctx = lax.axis_index("ctx")
    ch = lax.axis_index("ch")

    swap = []
    for h in range(2):
        for a in range(RING):
            for y in range(2):
                for z in range(RING):
                    there = h * RING + (z - a) % RING
                    swap.append((((h * RING + a) * 2 + y) * RING + z, (there * 2 + y) * RING + a))

    skip_row = skip[None, :]
    me = jnp.reshape(ctx, (1,)).astype(jnp.int32)
    smem = pl.BlockSpec(memory_space=pltpu.SMEM)
    cost = pl.CostEstimate(flops=4_000_000_000, bytes_accessed=4_000_000, transcendentals=0)
    params = lambda mib: pltpu.CompilerParams(vmem_limit_bytes=mib * MIB)
    lane = lambda *lead: pl.BlockSpec((*lead, LANES), lambda g: (*([0] * len(lead)), g))

    drive, segend, start, send, modes = pl.pallas_call(
        states_kernel,
        grid=(tiles,),
        in_specs=[
            pl.BlockSpec((1, tokens, LANES), lambda g: (1, 0, g)),
            pl.BlockSpec((1, tokens, LANES), lambda g: (2, 0, g)),
            pl.BlockSpec((1, 16, LANES), lambda g: (0, tokens // 16 - 1, g)),
            lane(3, 3),
            lane(MODES),
            lane(MODES),
        ],
        out_specs=[
            lane(tokens),
            lane(len(CHUNKS), MODES, SEGS),
            lane(len(CHUNKS), MODES),
            lane(CTX, ROWS),
            lane(2, MODES),
        ],
        out_shape=[
            jax.ShapeDtypeStruct((tokens, chans), F32),
            jax.ShapeDtypeStruct((len(CHUNKS), MODES, SEGS, chans), F32),
            jax.ShapeDtypeStruct((len(CHUNKS), MODES, chans), F32),
            jax.ShapeDtypeStruct((CTX, ROWS, chans), BF16),
            jax.ShapeDtypeStruct((2, MODES, chans), F32),
        ],
        scratch_shapes=[pltpu.VMEM((sum(room(n) for _, n in CHUNKS), LANES), F32)] * 2,
        compiler_params=params(60),
        cost_estimate=cost,
        name="states",
    )(streams, streams, streams, taps, decay.T, residues.T)
    w_block, modes = lax.optimization_barrier((w_out, modes))
    w_block = lax.ppermute(w_block, ("ctx", "ch"), swap)
    recv = lax.all_to_all(send, "ctx", 0, 0)

    def gate(group, entry):
        offset, size = CHUNKS[group[0]][0], sum(CHUNKS[c][1] for c in group)
        many, rest = len(group), len(CHUNKS) - len(group)
        q_spec = pl.BlockSpec((1, size, LANES), lambda g: (0, offset // size, g))
        shared_specs = [
            lane(3, 3),
            lane(2, MODES),
            lane(1),
            pl.BlockSpec((size, LANES), lambda g: (offset // size, g)),
            pl.BlockSpec((many, MODES, SEGS, LANES), lambda g: (group[0] // many, 0, 0, g)),
        ]
        shared = [taps, modes, skip_row, drive, segend]
        out_specs = [lane(CHUNKS[c][1]) for c in group]
        out_shape = [jax.ShapeDtypeStruct((CHUNKS[c][1], chans), BF16) for c in group]
        if group[0] == 0:
            in_specs = [smem, q_spec, *shared_specs, lane(len(CHUNKS), MODES), lane(CTX, ROWS)]
            args = [me, streams, *shared, start, recv]
            out_specs.append(lane(rest, MODES))
            out_shape.append(jax.ShapeDtypeStruct((rest, MODES, chans), F32))
        else:
            before = pl.BlockSpec((1, 16, LANES), lambda g: (0, offset // 16 - 1, g))
            in_specs = [q_spec, before, *shared_specs, lane(rest if many > rest else many, MODES)]
            args = [streams, streams, *shared, entry]
        return pl.pallas_call(
            functools.partial(gate_kernel, group, tokens),
            grid=(tiles,),
            in_specs=in_specs,
            out_specs=out_specs,
            out_shape=out_shape,
            scratch_shapes=[pltpu.VMEM((sum(room(CHUNKS[c][1]) for c in group), LANES), F32)] * 2,
            compiler_params=params(60),
            cost_estimate=cost,
            name="gate",
        )(*args)

    up = [(y * RING + z, y * RING + (z + 1) % RING) for y in range(2) for z in range(RING)]
    down = [(d, s) for s, d in up]
    across = [(i, (i + RING) % CH) for i in range(CH)]
    place = jnp.reshape(ch // RING, (1,)).astype(jnp.int32)

    *gated, entry = gate((0, 1), None)
    gated += gate((2,), entry)
    count = len(CHUNKS)
    arrived = {(c, 0, way): g for c, g in enumerate(gated) for way in "ud"}

    def hop(c, s, ways):
        for way in ways:
            block = arrived[c, s - 1, way]
            if s == RING // 2 and len(ways) == 2:
                half = block.shape[0] // 2
                block = block[half:] if way == "u" else block[:half]
            arrived[c, s, way] = lax.ppermute(block, "ch", up if way == "u" else down)

    def wait(c, s, d, t):
        for way in "ud":
            if (d, t, way) in arrived and (c, s - 1, way) in arrived:
                pair = arrived[d, t, way], arrived[c, s - 1, way]
                arrived[d, t, way], arrived[c, s - 1, way] = lax.optimization_barrier(pair)

    own = [None] * count
    theirs = [None] * count

    def weights(c, s, way):
        nonlocal w_all
        w, arrived[c, s, way] = lax.optimization_barrier((w_block, arrived[c, s, way]))
        w_all = lax.all_to_all(jnp.broadcast_to(w, (CTX, *w.shape)), "ctx", 0, 0)
        w_all = w_all.reshape(2, RING * chans, w.shape[1])

    def project(c):
        chunk = CHUNKS[c][1]
        rows = chunk // 2
        get = lambda way, *hops: [arrived[c, s, way] for s in hops if (c, s, way) in arrived]
        parts = [gated[c], *get("d", 1, 2, 3, 4), *get("u", 4, 3, 2, 1)]
        far = len(parts) - 7
        tile = pl.BlockSpec((rows, chans), lambda g: (g, 0))
        whole = pl.BlockSpec((rows, chans), lambda g: (0, 0))
        mine, other = pl.pallas_call(
            project_kernel,
            grid=(2,),
            in_specs=[smem] + [tile] * 4 + [[tile], [whole] * 2][far - 1] + [tile] * 3 + [pl.BlockSpec(w_all.shape, lambda g: (0,) * w_all.ndim)],
            out_specs=[tile] * 2,
            out_shape=[
                jax.ShapeDtypeStruct((chunk, chans), F32),
                jax.ShapeDtypeStruct((chunk, chans), BF16),
            ],
            compiler_params=params(20),
            cost_estimate=cost,
            name="project",
        )(place, *parts, w_all)
        return mine, other

    def send(c, mine, other):
        own[c], theirs[c] = mine, lax.ppermute(other, "ch", across)

    def ahead(k, c, s):
        mine, other = project(k)
        block = [arrived[c, s - 1, way] for way in "ud"]
        other, block = lax.optimization_barrier((other, block))
        arrived[c, s - 1, "u"], arrived[c, s - 1, "d"] = block
        send(k, mine, other)

    w_all = None
    steps = {"weights": weights, "hop": hop, "wait": wait, "ahead": ahead, "project": lambda c: send(c, *project(c))}
    for kind, *rest in PLAN:
        steps[kind](*rest)

    outs = [(mine + other.astype(F32)).astype(BF16) for mine, other in zip(own, theirs)]
    return jnp.concatenate(outs, axis=0)


def solution(mesh):
    return jax.shard_map(
        local,
        mesh=mesh,
        in_specs=(
            P(None, "ctx", "ch"),
            P(None, None, "ch"),
            P("ch", None),
            P("ch", None),
            P("ch"),
            P("ch", "ctx"),
        ),
        out_specs=P("ctx", "ch"),
        check_vma=False,
    )
```

```python
import functools

import jax
import jax.numpy as jnp
from jax import lax
from jax.experimental import pallas as pl
from jax.experimental.pallas import tpu as pltpu
from jax.sharding import PartitionSpec as P

MODES = 16
LANES = 128
SEGS = 8
CHUNKS = ((0, 512), (512, 512), (1024, 512))
ROWS = 48
CTX = 16
CH = 16
RING = 8
F32 = jnp.float32
BF16 = jnp.bfloat16
MIB = 1024 * 1024


PLAN = (
    ("weights", 1, 0, "u"),
    ("hop", 0, 1, "ud"),
    ("hop", 1, 1, "ud"),
    ("hop", 0, 2, "ud"),
    ("hop", 2, 1, "ud"),
    ("hop", 1, 2, "ud"),
    ("hop", 0, 3, "ud"),
    ("hop", 2, 2, "ud"),
    ("hop", 1, 3, "ud"),
    ("hop", 0, 4, "u"),
    ("hop", 2, 3, "ud"),
    ("hop", 1, 4, "d"),
    ("ahead", 0, 2, 4),
    ("hop", 2, 4, "ud"),
    ("project", 1),
    ("project", 2),
)


def row_ids():
    return lax.broadcasted_iota(jnp.int32, (SEGS, LANES), 0)


def wide(row):
    return jnp.broadcast_to(row, (SEGS, LANES))


def spread(ref, base, source, start, chunk):
    steps = chunk // SEGS
    for r in range(SEGS):
        at, row = base + r * (steps + 8), start + r * steps
        if row > 0:
            ref[pl.ds(at, steps + 8), :] = source[0, pl.ds(row - 16, steps + 16), :].astype(F32)[8:]
        else:
            ref[pl.ds(at + 8, steps), :] = source[0, pl.ds(0, steps), :].astype(F32)


def room(chunk):
    return chunk + SEGS * 8


def states_kernel(
    k_ref, v_ref, q_tail_ref, taps_ref, decay_ref, res_ref,
    drive_ref, segend_ref, start_ref, send_ref, modes_ref, kx, vx,
):
    tokens = k_ref.shape[1]
    kx[pl.ds(0, 8), :] = jnp.zeros((8, LANES), F32)
    vx[pl.ds(0, 8), :] = jnp.zeros((8, LANES), F32)
    decay = decay_ref[...]
    modes_ref[0] = decay
    modes_ref[1] = res_ref[...] * jnp.sqrt(decay)
    keep = jnp.exp(-decay)
    keeps = [wide(keep[m : m + 1]) for m in range(MODES)]
    tk = [wide(taps_ref[1, j : j + 1, :]) for j in range(3)]
    tv = [wide(taps_ref[2, j : j + 1, :]) for j in range(3)]
    later = (SEGS - 1 - row_ids()).astype(F32)
    state = jnp.zeros((MODES, LANES), F32)

    base = 0
    for c, (offset, chunk) in enumerate(CHUNKS):
        steps = chunk // SEGS
        spread(kx, base, k_ref, offset, chunk)
        spread(vx, base, v_ref, offset, chunk)

        def at(ref, i):
            return ref[pl.ds(base + 8 + i, SEGS, stride=steps + 8), :]

        def step(i, carry):
            k1, k2, v1, v2, acc = carry
            k0, v0 = at(kx, i), at(vx, i)
            keyed = tk[0] * k0 + tk[1] * k1 + tk[2] * k2
            valued = tv[0] * v0 + tv[1] * v1 + tv[2] * v2
            drive = keyed * valued
            drive_ref[pl.ds(pl.multiple_of(offset + i * SEGS, SEGS), SEGS), :] = drive
            return k0, k1, v0, v1, tuple(a * s + drive for a, s in zip(keeps, acc))

        zero = tuple(jnp.zeros((SEGS, LANES), F32) for _ in range(MODES))
        acc = lax.fori_loop(
            0, steps, step,
            (at(kx, -1), at(kx, -2), at(vx, -1), at(vx, -2), zero),
            unroll=16,
        )[4]
        start_ref[c] = state
        ends = []
        for m in range(MODES):
            segend_ref[c, m] = acc[m]
            weight = jnp.exp(-wide(decay[m : m + 1]) * (later * steps))
            ends.append(jnp.sum(acc[m] * weight, axis=0, keepdims=True))
        state = state * jnp.exp(-decay * chunk) + jnp.concatenate(ends, axis=0)
        base += room(chunk)

    tail = q_tail_ref.shape[1] - 2
    upper = state.astype(BF16).astype(F32)
    payload = jnp.concatenate(
        [
            upper,
            state - upper,
            kx[pl.ds(8, 2), :],
            vx[pl.ds(8, 2), :],
            q_tail_ref[0].astype(F32)[tail:],
            kx[pl.ds(base - 2, 2), :],
            vx[pl.ds(base - 2, 2), :],
            jnp.zeros((ROWS - 2 * MODES - 10, LANES), F32),
        ],
        axis=0,
    ).astype(BF16)
    for j in range(CTX):
        send_ref[j] = payload


def first_drive(taps_ref, heads, tails):
    short, full = [], []
    for s in (1, 2):
        t0, t1, t2 = (taps_ref[s, j : j + 1, :] for j in range(3))
        (x0, x1), (p2, p1) = heads[s - 1], tails[s - 1]
        short.append((t0 * x0, t0 * x1 + t1 * x0))
        full.append((short[-1][0] + t1 * p1 + t2 * p2, short[-1][1] + t2 * p1))
    return [full[0][i] * full[1][i] - short[0][i] * short[1][i] for i in range(2)]


def incoming_states(me, tokens, taps_ref, decay, recv_ref):
    span = jnp.exp(-decay * tokens)
    near = jnp.exp(-decay * (tokens - 1))
    next_to_near = jnp.exp(-decay * (tokens - 2))
    state = jnp.zeros((MODES, LANES), F32)
    extra = [jnp.zeros((1, LANES), F32)] * 2
    q_halo = jnp.zeros((2, LANES), F32)
    raw = [recv_ref[i, pl.ds(2 * MODES, 16), :].astype(F32) for i in range(CTX)]
    for i in range(CTX):
        ended = recv_ref[i, :MODES, :].astype(F32) + recv_ref[i, MODES : 2 * MODES, :].astype(F32)
        if i > 0:
            heads = [[raw[i][r : r + 1], raw[i][r + 1 : r + 2]] for r in (0, 2)]
            tails = [[raw[i - 1][r : r + 1], raw[i - 1][r + 1 : r + 2]] for r in (6, 8)]
            d0, d1 = first_drive(taps_ref, heads, tails)
            extra = [jnp.where(me == i, d, e) for d, e in zip((d0, d1), extra)]
            q_halo = jnp.where(me == i, raw[i - 1][4:6], q_halo)
            ended = ended + near * d0 + next_to_near * d1
        state = jnp.where(i < me, state * span + ended, state)
    return state, extra, q_halo


def gate_kernel(group, tokens, *refs):
    first = group[0] == 0
    if first:
        (me_ref, q_ref, taps_ref, modes_ref, skip_ref, drive_ref, segend_ref, start_ref, recv_ref) = refs[:9]
        out_refs = refs[9 : 9 + len(group)]
        (entry_ref, qx, gx) = refs[9 + len(group) :]
    else:
        (q_ref, qb_ref, taps_ref, modes_ref, skip_ref, drive_ref, segend_ref, entry_ref) = refs[:8]
        out_refs = refs[8 : 8 + len(group)]
        (qx, gx) = refs[8 + len(group) :]
    decay = modes_ref[0]
    extra = None
    if first:
        state, extra, q_halo = incoming_states(me_ref[0], tokens, taps_ref, decay, recv_ref)
        qx[pl.ds(6, 2), :] = q_halo
        entries = [state]
        for c in range(1, len(CHUNKS)):
            offset = CHUNKS[c][0]
            entries.append(
                jnp.exp(-decay * offset) * state
                + start_ref[c]
                + jnp.exp(-decay * (offset - 1)) * extra[0]
                + jnp.exp(-decay * (offset - 2)) * extra[1]
            )
            if c not in group:
                entry_ref[c - len(group)] = entries[c]
    else:
        before = qb_ref[0].astype(F32)
        qx[pl.ds(6, 2), :] = before[before.shape[0] - 2 :]
        entries = [entry_ref[k] for k in range(len(group))]
    keep = jnp.exp(-decay)
    scaled = modes_ref[1]
    rows = row_ids()
    keeps = [wide(keep[m : m + 1]) for m in range(MODES)]
    gains = [wide(scaled[m : m + 1]) for m in range(MODES)]
    tq = [wide(taps_ref[0, j : j + 1, :]) for j in range(3)]
    skip = wide(skip_ref[...])

    place = 0
    for k, c in enumerate(group):
        offset, chunk = CHUNKS[c]
        base = offset - CHUNKS[group[0]][0]
        steps = chunk // SEGS
        spread(qx, place, q_ref, base, chunk)
        keep1 = jnp.exp(-decay * steps)
        keep2 = jnp.exp(-decay * (2 * steps))
        keep4 = jnp.exp(-decay * (4 * steps))
        if c == 0:
            fix = jnp.exp(-decay * (steps - 1)) * extra[0] + jnp.exp(-decay * (steps - 2)) * extra[1]
        acc = []
        for m in range(MODES):
            ended = segend_ref[k, m]
            if c == 0:
                ended = ended + jnp.where(rows == 0, wide(fix[m : m + 1]), 0.0)
            x = jnp.where(rows == 0, wide(entries[k][m : m + 1]), pltpu.roll(ended, 1, 0))
            for far, factor in ((1, keep1), (2, keep2), (4, keep4)):
                moved = pltpu.roll(x, far, 0) * wide(factor[m : m + 1])
                x = x + jnp.where(rows >= far, moved, 0.0)
            acc.append(x)

        def at(i):
            return qx[pl.ds(place + 8 + i, SEGS, stride=steps + 8), :]

        def step(i, carry, more=None):
            q1, q2, acc = carry
            q0 = at(i)
            drive = drive_ref[pl.ds(pl.multiple_of(base + i * SEGS, SEGS), SEGS), :]
            if more is not None:
                drive = drive + jnp.where(rows == 0, wide(more), 0.0)
            acc = tuple(a * s + drive for a, s in zip(keeps, acc))
            terms = [g * s for g, s in zip(gains, acc)] + [skip * drive]
            while len(terms) > 1:
                terms = [sum(terms[i + 1 : i + 2], terms[i]) for i in range(0, len(terms), 2)]
            query = tq[0] * q0 + tq[1] * q1 + tq[2] * q2
            gx[pl.ds(place + i, SEGS, stride=steps + 8), :] = query * terms[0]
            return q0, q1, acc

        carry = (at(-1), at(-2), tuple(acc))
        begin = 0
        if c == 0:
            for begin in range(8):
                carry = step(begin, carry, extra[begin] if begin < 2 else None)
            begin = 8
        lax.fori_loop(begin, steps, step, carry, unroll=8)
        for r in range(SEGS):
            out_refs[k][pl.ds(r * steps, steps), :] = gx[pl.ds(place + r * (steps + 8), steps), :].astype(BF16)
        place += room(chunk)


def project_kernel(place_ref, *refs):
    *blocks, w_ref, own_ref, other_ref, rows_ref, sems = refs
    chunk, width = own_ref.shape
    half = chunk // 2
    column = lambda j: pl.ds(j * width, width)
    if len(blocks) == 9:
        wholes = [(j, blocks[j if j < 4 else j + 1]) for j in range(RING) if j != 4]
        copies = [(blocks[4 + i], rows_ref.at[pl.ds(i * half, half), column(4)]) for i in range(2)]
    else:
        wholes, copies = list(enumerate(blocks)), []
    copies += [(block, rows_ref.at[:, column(j)]) for j, block in wholes]
    copies = [pltpu.make_async_copy(a, b, sems.at[i]) for i, (a, b) in enumerate(copies)]
    for copy in copies:
        copy.start()
    for copy in copies:
        copy.wait()
    side = place_ref[0]
    for i in range(2):
        at = pl.ds(i * half, half)
        rows = rows_ref[at, :]
        own_ref[at, :] = jnp.dot(rows, w_ref[side], preferred_element_type=F32)
        other_ref[at, :] = jnp.dot(rows, w_ref[1 - side], preferred_element_type=F32).astype(BF16)


def local(streams, taps, residues, decay, skip, w_out):
    tokens, chans = streams.shape[1], streams.shape[2]
    tiles = chans // LANES
    ctx = lax.axis_index("ctx")
    ch = lax.axis_index("ch")

    swap = []
    for h in range(2):
        for a in range(RING):
            for y in range(2):
                for z in range(RING):
                    there = h * RING + (z - a) % RING
                    swap.append((((h * RING + a) * 2 + y) * RING + z, (there * 2 + y) * RING + a))

    skip_row = skip[None, :]
    me = jnp.reshape(ctx, (1,)).astype(jnp.int32)
    smem = pl.BlockSpec(memory_space=pltpu.SMEM)
    cost = pl.CostEstimate(flops=4_000_000_000, bytes_accessed=4_000_000, transcendentals=0)
    params = lambda mib: pltpu.CompilerParams(vmem_limit_bytes=mib * MIB)
    lane = lambda *lead: pl.BlockSpec((*lead, LANES), lambda g: (*([0] * len(lead)), g))

    drive, segend, start, send, modes = pl.pallas_call(
        states_kernel,
        grid=(tiles,),
        in_specs=[
            pl.BlockSpec((1, tokens, LANES), lambda g: (1, 0, g)),
            pl.BlockSpec((1, tokens, LANES), lambda g: (2, 0, g)),
            pl.BlockSpec((1, 16, LANES), lambda g: (0, tokens // 16 - 1, g)),
            lane(3, 3),
            lane(MODES),
            lane(MODES),
        ],
        out_specs=[
            lane(tokens),
            lane(len(CHUNKS), MODES, SEGS),
            lane(len(CHUNKS), MODES),
            lane(CTX, ROWS),
            lane(2, MODES),
        ],
        out_shape=[
            jax.ShapeDtypeStruct((tokens, chans), F32),
            jax.ShapeDtypeStruct((len(CHUNKS), MODES, SEGS, chans), F32),
            jax.ShapeDtypeStruct((len(CHUNKS), MODES, chans), F32),
            jax.ShapeDtypeStruct((CTX, ROWS, chans), BF16),
            jax.ShapeDtypeStruct((2, MODES, chans), F32),
        ],
        scratch_shapes=[pltpu.VMEM((sum(room(n) for _, n in CHUNKS), LANES), F32)] * 2,
        compiler_params=params(60),
        cost_estimate=cost,
        name="states",
    )(streams, streams, streams, taps, decay.T, residues.T)
    w_block, modes = lax.optimization_barrier((w_out, modes))
    w_block = lax.ppermute(w_block, ("ctx", "ch"), swap)
    recv = lax.all_to_all(send, "ctx", 0, 0)

    def gate(group, entry):
        offset, size = CHUNKS[group[0]][0], sum(CHUNKS[c][1] for c in group)
        many, rest = len(group), len(CHUNKS) - len(group)
        q_spec = pl.BlockSpec((1, size, LANES), lambda g: (0, offset // size, g))
        shared_specs = [
            lane(3, 3),
            lane(2, MODES),
            lane(1),
            pl.BlockSpec((size, LANES), lambda g: (offset // size, g)),
            pl.BlockSpec((many, MODES, SEGS, LANES), lambda g: (group[0] // many, 0, 0, g)),
        ]
        shared = [taps, modes, skip_row, drive, segend]
        out_specs = [lane(CHUNKS[c][1]) for c in group]
        out_shape = [jax.ShapeDtypeStruct((CHUNKS[c][1], chans), BF16) for c in group]
        if group[0] == 0:
            in_specs = [smem, q_spec, *shared_specs, lane(len(CHUNKS), MODES), lane(CTX, ROWS)]
            args = [me, streams, *shared, start, recv]
            out_specs.append(lane(rest, MODES))
            out_shape.append(jax.ShapeDtypeStruct((rest, MODES, chans), F32))
        else:
            before = pl.BlockSpec((1, 16, LANES), lambda g: (0, offset // 16 - 1, g))
            in_specs = [q_spec, before, *shared_specs, lane(rest if many > rest else many, MODES)]
            args = [streams, streams, *shared, entry]
        return pl.pallas_call(
            functools.partial(gate_kernel, group, tokens),
            grid=(tiles,),
            in_specs=in_specs,
            out_specs=out_specs,
            out_shape=out_shape,
            scratch_shapes=[pltpu.VMEM((sum(room(CHUNKS[c][1]) for c in group), LANES), F32)] * 2,
            compiler_params=params(60),
            cost_estimate=cost,
            name="gate",
        )(*args)

    up = [(y * RING + z, y * RING + (z + 1) % RING) for y in range(2) for z in range(RING)]
    down = [(d, s) for s, d in up]
    across = [(i, (i + RING) % CH) for i in range(CH)]
    place = jnp.reshape(ch // RING, (1,)).astype(jnp.int32)

    *gated, entry = gate((0, 1), None)
    gated += gate((2,), entry)
    count = len(CHUNKS)
    arrived = {(c, 0, way): g for c, g in enumerate(gated) for way in "ud"}

    def hop(c, s, ways):
        for way in ways:
            block = arrived[c, s - 1, way]
            if s == RING // 2 and len(ways) == 2:
                half = block.shape[0] // 2
                block = block[half:] if way == "u" else block[:half]
            arrived[c, s, way] = lax.ppermute(block, "ch", up if way == "u" else down)

    def wait(c, s, d, t):
        for way in "ud":
            if (d, t, way) in arrived and (c, s - 1, way) in arrived:
                pair = arrived[d, t, way], arrived[c, s - 1, way]
                arrived[d, t, way], arrived[c, s - 1, way] = lax.optimization_barrier(pair)

    own = [None] * count
    theirs = [None] * count

    def weights(c, s, way):
        nonlocal w_all
        w, arrived[c, s, way] = lax.optimization_barrier((w_block, arrived[c, s, way]))
        w_all = lax.all_to_all(jnp.broadcast_to(w, (CTX, *w.shape)), "ctx", 0, 0)
        w_all = w_all.reshape(2, RING * chans, w.shape[1])

    def project(c):
        chunk = CHUNKS[c][1]
        get = lambda way, *hops: [arrived[c, s, way] for s in hops if (c, s, way) in arrived]
        parts = [gated[c], *get("d", 1, 2, 3, 4), *get("u", 4, 3, 2, 1)]
        vmem = pl.BlockSpec(memory_space=pltpu.VMEM)
        mine, other = pl.pallas_call(
            project_kernel,
            in_specs=[smem] + [pl.BlockSpec(memory_space=pltpu.HBM)] * len(parts) + [vmem],
            out_specs=[vmem] * 2,
            out_shape=[
                jax.ShapeDtypeStruct((chunk, chans), F32),
                jax.ShapeDtypeStruct((chunk, chans), BF16),
            ],
            scratch_shapes=[
                pltpu.VMEM((chunk, RING * chans), BF16),
                pltpu.SemaphoreType.DMA((len(parts),)),
            ],
            compiler_params=params(10),
            cost_estimate=cost,
            name="project",
        )(place, *parts, w_all)
        return mine, other

    def send(c, mine, other):
        own[c], theirs[c] = mine, lax.ppermute(other, "ch", across)

    def ahead(k, c, s):
        mine, other = project(k)
        block = [arrived[c, s - 1, way] for way in "ud"]
        other, block = lax.optimization_barrier((other, block))
        arrived[c, s - 1, "u"], arrived[c, s - 1, "d"] = block
        send(k, mine, other)

    w_all = None
    steps = {"weights": weights, "hop": hop, "wait": wait, "ahead": ahead, "project": lambda c: send(c, *project(c))}
    for kind, *rest in PLAN:
        steps[kind](*rest)

    outs = [(mine + other.astype(F32)).astype(BF16) for mine, other in zip(own, theirs)]
    return jnp.concatenate(outs, axis=0)


def solution(mesh):
    return jax.shard_map(
        local,
        mesh=mesh,
        in_specs=(
            P(None, "ctx", "ch"),
            P(None, None, "ch"),
            P("ch", None),
            P("ch", None),
            P("ch"),
            P("ch", "ctx"),
        ),
        out_specs=P("ctx", "ch"),
        check_vma=False,
    )
```
